512 devices in a mesh: row: 32 (over x, y), col: 16 (over z, core).
Axes of the slice: x: 4, y: 8, z: 8, core: 2. Of those that a mesh axis runs over, the one named last changes fastest.
Arguments:
- embeddings: float32 [64, 32768], P(None, 'col'), may hold values from -0.75 to 0.75
- confidence: bfloat16 [32768, 32768], P('row', 'col'), may hold values from 0.049804688 to 1
- sketch: float32 [40, 32768], P(None, 'col'), may hold values from -6 to 6
Outputs:
- basis: float32 [40, 32768], P(None, 'row')
- r_factor: float32 [40, 40], replicated
The draws below stay inside these ranges and needn't reach their ends.
All inputs are finite; a program needn't handle non-finite values.
Results may differ from the reference program's by a relative error of at most 0.0003.
Values sent between devices are 32-bit elements; how exact they have to be, the bound alone decides.
No kernel may reach another device: no remote copies, remote signals or barrier semaphores. Data moves between devices by JAX's collectives and lax.ppermute only.
A program may use at most 64 MiB of HBM per device.

```python
import math
import jax
import jax.numpy as jnp
from jax import lax

E = 64
K = 40
ROW_DEV = 1024
NPTS = 32768
N_ROW = 32


def levels(own_key, dims, pieces, least, high):
    loudness, own = 1.0, jax.random.fold_in(own_key, 6)
    for axis_at, shards_of in pieces:
        steps = jnp.exp(jax.random.uniform(jax.random.fold_in(own, axis_at), (shards_of,), jnp.float32, least / len(pieces), high / len(pieces)))
        loudness = loudness * jnp.repeat(steps, dims[axis_at] // shards_of).reshape([-1 if axis == axis_at else 1 for axis in range(len(dims))])
    return loudness


def noise(rng, dims, width, most, pieces=(), held_as=jnp.bfloat16):
    entries = jax.random.normal(rng, dims, jnp.float32) * width
    if len(pieces) > 0:
        entries = levels(rng, dims, pieces, -0.22, 0.18) * entries
    return jnp.clip(entries, min=-most, max=most).astype(held_as)


def setup_inputs(seed: int = 0) -> dict:
    seeds = jax.random.split(jax.random.key(seed), 4)
    return {
        "embeddings": noise(seeds[0], (E, NPTS), 0.125, 0.75, ((1, 16),), jnp.float32),
        "confidence": jnp.clip(jnp.exp(math.log(1.0) - 2.9996462 * jax.random.uniform(seeds[1], (NPTS, NPTS), jnp.float32) ** levels(seeds[1], (NPTS, NPTS), ((0, 32), (1, 16)), -0.2, 0.2)), 0.049804688, 1.0).astype(jnp.bfloat16),
        "sketch": noise(seeds[2], (K, NPTS), 1.0, 6.0, ((1, 16),), jnp.float32),
    }


HIGHEST_PRECISION = lax.Precision.HIGHEST

def reference(embeddings, confidence, sketch):
    norms_all = lax.optimization_barrier(jnp.sum(embeddings * embeddings, axis=0))
    sketch_mean = lax.optimization_barrier(jnp.sum(sketch, axis=1)) / NPTS
    centred = sketch - sketch_mean[:, None]

    def row_block(offset):
        points = lax.dynamic_slice_in_dim(embeddings, offset, ROW_DEV, 1)
        norms_here = lax.dynamic_slice_in_dim(norms_all, offset, ROW_DEV, 0)
        weights = lax.dynamic_slice_in_dim(confidence, offset, ROW_DEV, 0).astype(jnp.float32)
        inner_prod = lax.dot_general(points.astype(jnp.float32), embeddings.astype(jnp.float32), (((0,), (0,)), ((), ())), precision=HIGHEST_PRECISION, preferred_element_type=jnp.float32)
        distance = norms_here[:, None] + norms_all[None, :] - 2.0 * inner_prod
        weighted = weights * distance
        return lax.dot_general(centred.astype(jnp.float32), weighted.astype(jnp.float32), (((1,), (1,)), ((), ())), precision=HIGHEST_PRECISION, preferred_element_type=jnp.float32)
    offsets = (jnp.arange(N_ROW) * ROW_DEV).astype(jnp.int32)
    blocks = lax.map(row_block, offsets)
    product = jnp.transpose(blocks, (1, 0, 2)).reshape(K, NPTS)
    row_mean = lax.optimization_barrier(jnp.sum(product, axis=1)) / NPTS
    lowered = -0.5 * (product - row_mean[:, None])
    q_factor, upper_tri = jnp.linalg.qr(lowered.T)
    diag_signs = jnp.sign(jnp.diagonal(upper_tri))
    basis = jnp.sqrt(jnp.float32(NPTS)) * (q_factor * diag_signs[None, :]).T
    scaled = upper_tri * diag_signs[:, None] / NPTS
    return (basis, scaled)
```

```python
import math

import jax
import jax.numpy as jnp
from jax import lax
from jax.sharding import PartitionSpec as P

HIGHEST_PRECISION = lax.Precision.HIGHEST


def contract_last(left, right):
    return lax.dot_general(
        left,
        right,
        (((1,), (1,)), ((), ())),
        precision=HIGHEST_PRECISION,
        preferred_element_type=jnp.float32,
    )


def cholesky_pass(gram_matrix, block_rows):
    factor_low = jnp.linalg.cholesky(gram_matrix)
    solved = lax.linalg.triangular_solve(factor_low, block_rows, left_side=True, lower=True)
    return (solved, factor_low.T)


def exchange(blocks, axis):
    return lax.all_to_all(blocks, axis, split_axis=0, concat_axis=0, tiled=True)


def share(block, axis):
    return exchange(jnp.broadcast_to(block[None], (lax.axis_size(axis),) + block.shape), axis)


def doubling_sum(block, axis):
    size = lax.axis_size(axis)
    step = 1
    while step < size:
        block = block + lax.ppermute(block, axis, [(i, i ^ step) for i in range(size)])
        step *= 2
    return block


def local(embeddings, confidence, sketch):
    n_row, n_col = lax.axis_size("row"), lax.axis_size("col")
    row_dev, col_dev = confidence.shape
    count_all = row_dev * n_row
    halves = col_dev // row_dev
    piece = row_dev // n_col
    k = sketch.shape[0]
    rindex = lax.axis_index("row")

    half = lax.dynamic_slice_in_dim(embeddings, (rindex % halves) * row_dev, row_dev, 1)
    mine = lax.dynamic_slice_in_dim(half, (rindex // halves) * piece, piece, 1)
    pairs = [
        (r * n_col + c, (c * halves + r % halves) * n_col + r // halves)
        for r in range(n_row)
        for c in range(n_col)
    ]
    piece_points = lax.ppermute(mine, ("row", "col"), pairs)
    points = jnp.transpose(share(piece_points, "col"), (1, 0, 2)).reshape(-1, row_dev)

    norms_col = jnp.sum(embeddings * embeddings, axis=0)
    norms_row = jnp.sum(points * points, axis=0)
    inner_prod = lax.dot_general(
        points,
        embeddings,
        (((0,), (0,)), ((), ())),
        precision=HIGHEST_PRECISION,
        preferred_element_type=jnp.float32,
    )
    distance = norms_row[:, None] + norms_col[None, :] - 2.0 * inner_prod
    weighted = confidence.astype(jnp.float32) * distance

    mean_here = jnp.sum(sketch, axis=1) / col_dev
    centred = sketch - mean_here[:, None]
    part = contract_last(jnp.concatenate([centred, jnp.ones((1, col_dev), jnp.float32)], 0), weighted)
    cut = jnp.transpose(part.reshape(k + 1, n_col, piece), (1, 0, 2))
    means = jnp.broadcast_to(jnp.pad(mean_here, (0, piece - k))[None, None, :], (n_col, 1, piece))
    got = exchange(jnp.concatenate([cut, means], axis=1), "col")
    mean_blocks = got[:, k + 1, :k]
    shift = mean_blocks - jnp.sum(mean_blocks, axis=0) / n_col
    product_piece = jnp.sum(got[:, :k] + shift[:, :, None] * got[:, k : k + 1], axis=0)
    product = jnp.transpose(share(product_piece, "col"), (1, 0, 2)).reshape(k, row_dev)

    mean_rows = jnp.sum(product, axis=1, keepdims=True) / row_dev
    from_mean = product - mean_rows
    gram = contract_last(from_mean, from_mean)
    all_rows = share(jnp.concatenate([gram, mean_rows.T], axis=0), "row")
    row_means = all_rows[:, k]
    row_mean = jnp.sum(row_means, axis=0) / n_row
    off = row_means - row_mean
    between = lax.dot_general(
        off, off, (((0,), (0,)), ((), ())), precision=HIGHEST_PRECISION, preferred_element_type=jnp.float32
    )
    gram_all = 0.25 * (jnp.sum(all_rows[:, :k], axis=0) + row_dev * between)
    lowered = -0.5 * (product - row_mean[:, None])
    basis_one, upper_one = cholesky_pass(gram_all, lowered)
    gram_two = doubling_sum(contract_last(basis_one, basis_one), "row")
    basis_two, upper_two = cholesky_pass(gram_two, basis_one)
    upper_tri = jnp.dot(upper_two, upper_one, precision=HIGHEST_PRECISION)
    basis = math.sqrt(count_all) * basis_two
    return (basis, upper_tri / count_all)


def solution(mesh):
    placed = (P(None, "col"), P("row", "col"), P(None, "col"))
    return jax.shard_map(
        local, mesh=mesh, in_specs=placed, out_specs=(P(None, "row"), P()), check_vma=False
    )
```

```python
import functools
import math

import jax
import jax.numpy as jnp
from jax import lax
from jax.experimental import pallas as pl
from jax.experimental.pallas import tpu as pltpu
from jax.sharding import PartitionSpec as P

HIGHEST_PRECISION = lax.Precision.HIGHEST
ROW, COL = ("x", "y"), ("z", "core")
LANES = 128
HALF = 64
PACK = 24
ONES = 40
INV = 48
STEP = 256
VMEM = 48 * 1024 * 1024


def dot(left, right, contract, precision=None):
    return lax.dot_general(
        left, right, ((contract[0], contract[1]), ((), ())), precision=precision, preferred_element_type=jnp.float32
    )


def lane_of(shape):
    return lax.broadcasted_iota(jnp.int32, shape, len(shape) - 1)


def row_of(shape):
    return lax.broadcasted_iota(jnp.int32, shape, len(shape) - 2)


def halves_of(values):
    high = values.astype(jnp.bfloat16).astype(jnp.float32)
    return high, values - high


def thirds_of(values):
    first, rest = halves_of(values)
    second, third = halves_of(rest)
    return first, second, third


def one_of(index, choices, other):
    for at, choice in choices.items():
        other = jnp.where(index == at, choice, other)
    return other


def columns_kernel(count, emb_ref, sketch_ref, points_ref, sketch_t_ref, shift_ref, mean_ref):
    emb = emb_ref[...]
    wide = emb.shape[1]
    shift = jnp.sum(emb, axis=1, keepdims=True) * (1.0 / wide)
    shift_ref[...] = jnp.broadcast_to(shift, shift_ref.shape)
    moved = emb - shift
    high, low = halves_of(moved)
    norms = jnp.sum(moved * moved, axis=0, keepdims=True)
    first, second, third = thirds_of(norms)
    at = row_of((16, wide))
    tail = one_of(at, {0: 1.0, 1: 1.0, 2: 1.0, 3: first, 4: second, 5: third}, 0.0)
    points_ref[...] = jnp.concatenate([high, high, low, tail], axis=0).astype(jnp.bfloat16)

    sketch = sketch_ref[...]
    mean = jnp.sum(sketch, axis=1, keepdims=True) * (1.0 / wide)
    high, low = halves_of(sketch - mean)
    ones = jnp.where(row_of((8, wide)) == 0, 1.0, 0.0)
    both = jnp.concatenate([high, ones, low, jnp.zeros((LANES - 88, wide), jnp.float32)], axis=0)
    sketch_t_ref[...] = both.T.astype(jnp.bfloat16)
    across = jnp.concatenate(
        [jnp.broadcast_to(mean, (mean.shape[0], LANES)), jnp.zeros((LANES - mean.shape[0], LANES), jnp.float32)], axis=0
    )
    mean_ref[...] = across.T[:8]


def product_kernel(rows_ref, conf_ref, points_ref, sketch_t_ref, shift_ref, mean_ref, out_ref):
    emb = rows_ref[...].reshape(HALF, STEP)
    moved = emb - shift_ref[:, :1]
    norms = jnp.sum(moved * moved, axis=0, keepdims=True)
    first, second, third = thirds_of(norms)
    high, low = halves_of(-2.0 * moved)
    tail = one_of(row_of((HALF, STEP)), {0: first, 1: second, 2: third, 3: 1.0, 4: 1.0, 5: 1.0}, 0.0)
    left = jnp.concatenate([high, low, high, tail], axis=0).T.astype(jnp.bfloat16)[:, :208]
    total = jnp.zeros((STEP, LANES), jnp.float32)
    wide = conf_ref.shape[1]
    for start in range(0, wide, 256):
        part = slice(start, start + 256)
        distance = dot(left, points_ref[:, part], ((1,), (0,)))
        weighted = conf_ref[:, part].astype(jnp.float32) * distance
        high = weighted.astype(jnp.bfloat16)
        low = (weighted - high.astype(jnp.float32)).astype(jnp.bfloat16)
        right = sketch_t_ref[part, :]
        total = total + dot(high, right, ((1,), (0,))) + dot(low, right, ((1,), (0,)))
    flat = total.T
    flat = flat[:48] + flat[48:96]
    shape = (PACK, LANES)
    lane, row = lane_of(shape), row_of(shape)
    means = jnp.broadcast_to(pltpu.roll(mean_ref[...], HALF, 1)[:1], shape)
    is_mean = (row == ONES + 1 - PACK) & (lane >= HALF)
    for tile in range(STEP // LANES):
        top = flat[:PACK, tile * LANES : (tile + 1) * LANES]
        bottom = flat[PACK:, tile * LANES : (tile + 1) * LANES]
        even = jnp.where(lane < HALF, top, pltpu.roll(bottom, HALF, 1))
        odd = jnp.where(lane < HALF, pltpu.roll(top, HALF, 1), bottom)
        out_ref[2 * tile] = jnp.where(is_mean, means, even)
        out_ref[2 * tile + 1] = jnp.where(is_mean, means, odd)


def piece_kernel(got_ref, out_ref):
    total = got_ref[0]
    for block in range(1, got_ref.shape[0]):
        total = total + got_ref[block]
    sums = pltpu.roll(got_ref[:, ONES - PACK, :], HALF, 1)
    means = pltpu.roll(got_ref[:, ONES + 1 - PACK, :], HALF, 1)
    means = means - jnp.sum(means, axis=0, keepdims=True) * (1.0 / means.shape[0])
    fix = dot(means.T, sums, ((1,), (0,)), HIGHEST_PRECISION)
    shape = (PACK, LANES)
    lane, row = lane_of(shape), row_of(shape)
    total = total + jnp.where(lane < HALF, fix[:PACK], pltpu.roll(fix[PACK : 2 * PACK], HALF, 1))
    below = (lane >= HALF) & (row >= ONES - PACK)
    total = jnp.where(below, jnp.where(row == ONES - PACK, 1.0, 0.0), total)
    out_ref[...] = jnp.broadcast_to(total[None], out_ref.shape)


def unpack(pieces_ref):
    lane = lane_of((PACK, LANES))
    tops, bottoms = [], []
    for at in range(0, pieces_ref.shape[0], 2):
        even, odd = pieces_ref[at], pieces_ref[at + 1]
        tops.append(jnp.where(lane < HALF, even, pltpu.roll(odd, HALF, 1)))
        bottoms.append(jnp.where(lane < HALF, pltpu.roll(even, HALF, 1), odd))
    return jnp.concatenate([jnp.concatenate(tops, axis=1), jnp.concatenate(bottoms, axis=1)], axis=0)


def gram_kernel(pieces_ref, out_ref):
    product = unpack(pieces_ref)
    padded = jnp.concatenate([product, jnp.zeros((LANES - 48, product.shape[1]), jnp.float32)], axis=0)
    gram = dot(product, padded, ((1,), (1,)), HIGHEST_PRECISION)
    lane = lane_of((8, LANES))
    packed = jnp.zeros((8, LANES), jnp.float32)
    for group in range(5):
        rows = gram[8 * group : 8 * group + 8]
        lower = jnp.where(lane < 8 * group + 8, rows, 0.0)
        packed = packed + (pltpu.roll(lower, 4 * group * (group + 1), 1) if group else lower)
        packed = packed + pltpu.roll(jnp.where(lane == ONES, rows, 0.0), 120 + group - ONES, 1)
    out_ref[...] = jnp.broadcast_to(packed[None], out_ref.shape)


def spread_lane(rows, at):
    return jnp.broadcast_to(rows[:, at : at + 1], (8, LANES))


def spread_row(rows, at):
    return jnp.broadcast_to(rows[at : at + 1, :], (8, LANES))


def factor_kernel(count, grams_ref, pieces_ref, basis_ref, upper_ref, bound_ref):
    packed = grams_ref[0]
    for block in range(1, grams_ref.shape[0]):
        packed = packed + grams_ref[block]
    shape = (8, LANES)
    lane, row = lane_of(shape), row_of(shape)
    lowers, sums = [], []
    for group in range(5):
        back = (LANES - 4 * group * (group + 1)) % LANES
        lower = pltpu.roll(packed, back, 1) if back else packed
        lowers.append(jnp.where(lane < 8 * group + 8, lower, 0.0))
        sums.append(jnp.where(lane == ONES, pltpu.roll(packed, LANES + ONES - 120 - group, 1), 0.0))
    square = jnp.concatenate([a + b for a, b in zip(lowers, sums)] + [jnp.zeros((LANES - 40, LANES), jnp.float32)], axis=0)
    flipped = square.T
    ones_row = jnp.where(lane < ONES, spread_row(flipped[ONES : ONES + 8], 0), jnp.where(lane == INV + ONES, 1.0, 0.0))
    groups, trace = [], jnp.zeros((8, 1), jnp.float32)
    for group in range(5):
        upper = jnp.where((lane >= 8 * group + 8) & (lane < ONES), flipped[8 * group : 8 * group + 8], 0.0)
        full = lowers[group] + upper
        diagonal = lane == 8 * group + row
        trace = trace + jnp.sum(jnp.where(diagonal, full, 0.0), axis=1, keepdims=True)
        full = full + jnp.where(lane == INV + 8 * group + row, 1.0, 0.0)
        groups.append(full - (spread_lane(sums[group], ONES) * (1.0 / count)) * ones_row)

    size = jnp.zeros((8, 1), jnp.float32)
    scaled = []
    for block in range(5):
        base = 8 * block
        columns = {i: [spread_lane(groups[i], base + t) for t in range(8)] for i in range(block, 5)}
        rows = [spread_row(groups[block], t) for t in range(8)]
        entry = {(t, s): spread_row(columns[block][s], t) for t in range(8) for s in range(t, 8)}
        result = jnp.zeros(shape, jnp.float32)
        for t in range(8):
            inverse = 1.0 / entry[t, t]
            for s in range(t + 1, 8):
                factor = entry[t, s] * inverse
                for u in range(s, 8):
                    entry[s, u] = entry[s, u] - factor * entry[t, u]
                rows[s] = rows[s] - factor * rows[t]
            for i in range(block + 1, 5):
                factor = columns[i][t] * inverse
                for s in range(t + 1, 8):
                    columns[i][s] = columns[i][s] - factor * entry[t, s]
                groups[i] = groups[i] - factor * rows[t]
            result = jnp.where(row == t, rows[t] * lax.rsqrt(entry[t, t]), result)
        scaled.append(result)
        kept = (lane >= INV) & (lane < INV + ONES)
        size = size + jnp.sum(jnp.where(kept, result * result, 0.0), axis=1, keepdims=True)
        triangle = jnp.where(lane >= base + row, result, 0.0) * (0.5 / count)
        upper_ref[base : base + 8, :] = triangle[:, :40]
    bound = jnp.sum(trace, axis=0, keepdims=True) * jnp.sum(size, axis=0, keepdims=True)
    bound_ref[...] = jnp.broadcast_to(bound, shape)
    solve = jnp.concatenate(scaled, axis=0) * -math.sqrt(count)
    solve = pltpu.roll(solve, LANES - INV, 1)[:, :48]
    basis_ref[...] = dot(solve, unpack(pieces_ref), ((1,), (0,)), HIGHEST_PRECISION)


def call(kernel, outs, flops, *args, **more):
    moved = sum(math.prod(a.shape) * a.dtype.itemsize for a in (*args, *outs))
    return pl.pallas_call(
        kernel,
        out_shape=outs,
        compiler_params=pltpu.CompilerParams(vmem_limit_bytes=VMEM),
        cost_estimate=pl.CostEstimate(flops=flops, bytes_accessed=moved, transcendentals=0),
        **more,
    )(*args)


def array(*shape, dtype=jnp.float32):
    return jax.ShapeDtypeStruct(shape, dtype)


def columns_side(embeddings, sketch):
    wide = embeddings.shape[1]
    outs = (
        array(208, wide, dtype=jnp.bfloat16),
        array(wide, LANES, dtype=jnp.bfloat16),
        array(64, LANES),
        array(8, LANES),
    )
    return call(functools.partial(columns_kernel, wide), outs, 10_000_000, embeddings, sketch)


def product_pieces(rows, confidence, sides):
    row_dev, wide = confidence.shape
    steps = row_dev // STEP
    whole = lambda a: pl.BlockSpec(a.shape, lambda i: (0,) * a.ndim)
    return call(
        product_kernel,
        (array(row_dev // HALF, PACK, LANES),),
        2 * row_dev * wide * (256 + 2 * LANES),
        rows,
        confidence,
        *sides,
        grid=(steps,),
        in_specs=[
            pl.BlockSpec((8, 1, 8, STEP), lambda i: (0, i // 2, 0, i % 2)),
            pl.BlockSpec((STEP, wide), lambda i: (i, 0)),
            *[whole(a) for a in sides],
        ],
        out_specs=(pl.BlockSpec((STEP // HALF, PACK, LANES), lambda i: (i, 0, 0)),),
    )[0]


def piece_sum(got):
    return call(piece_kernel, (array(*got.shape),), 1_000_000, got)[0]


def gram_tile(pieces, copies):
    return call(gram_kernel, (array(copies, 8, LANES),), 40_000_000, pieces)[0]


def factored(grams, pieces, count):
    points = pieces.shape[0] * HALF
    outs = (array(40, points), array(40, 40), array(8, LANES))
    return call(functools.partial(factor_kernel, count), outs, 40_000_000, grams, pieces)


def exchange(blocks, axis):
    return lax.all_to_all(blocks, axis, split_axis=0, concat_axis=0, tiled=True)


def local(embeddings, confidence, sketch):
    n_row, n_col = lax.axis_size(ROW), lax.axis_size(COL)
    row_dev, col_dev = confidence.shape
    count = row_dev * n_row
    halves = col_dev // row_dev
    rindex = lax.axis_index(ROW)

    dims, points = embeddings.shape[0] * 2 // n_col, row_dev // 2
    target = rindex // halves
    mine = lax.dynamic_slice(
        embeddings, (target // 2 * dims, rindex % halves * row_dev + target % 2 * points), (dims, points)
    )
    pairs = [
        (r * n_col + c, (c * halves + r % halves) * n_col + r // halves)
        for r in range(n_row)
        for c in range(n_col)
    ]
    piece = lax.ppermute(mine, ROW + COL, pairs)
    rows = exchange(jnp.broadcast_to(piece[None], (n_col, dims, points)), COL).reshape(-1, 2, dims, points)

    partial_pieces = product_pieces(rows, confidence, columns_side(embeddings, sketch))
    pieces = exchange(piece_sum(exchange(partial_pieces, COL)), COL)
    grams = exchange(gram_tile(pieces, n_row), ROW)
    basis, upper_tri, bound = factored(grams, pieces, count)

    def one_pass():
        return basis, upper_tri

    def two_passes():
        gram = lax.psum(dot(basis, basis, ((1,), (1,)), HIGHEST_PRECISION), ROW) / count
        factor_low = jnp.linalg.cholesky(gram)
        solved = lax.linalg.triangular_solve(factor_low, basis, left_side=True, lower=True)
        return solved, jnp.dot(factor_low.T, upper_tri, precision=HIGHEST_PRECISION)

    return lax.cond(bound[0, 0] < 2.5 * 40 * 40, one_pass, two_passes)


def solution(mesh):
    chips = jax.sharding.Mesh(mesh.devices.reshape(4, 8, 8, 2), ROW + COL)
    placed = (P(None, COL), P(ROW, COL), P(None, COL))
    return jax.shard_map(
        local, mesh=chips, in_specs=placed, out_specs=(P(None, ROW), P()), check_vma=False
    )
```

```python
import functools
import itertools
import math

import jax
import jax.numpy as jnp
from jax import lax
from jax.experimental import pallas as pl
from jax.experimental.pallas import tpu as pltpu
from jax.sharding import PartitionSpec as P

HIGHEST_PRECISION = lax.Precision.HIGHEST
ROW, NEAR = ("x", "y"), ("z_low", "core")
COL = ("z_high",) + NEAR
LANES = 128
HALF = 64
PACK = 24
ONES = 40
INV = 48
STEP = 512
CHUNK = 256
VMEM = 32 * 1024 * 1024


def dot(left, right, contract, precision=None):
    return lax.dot_general(
        left, right, ((contract[0], contract[1]), ((), ())), precision=precision, preferred_element_type=jnp.float32
    )


def lane_of(shape):
    return lax.broadcasted_iota(jnp.int32, shape, len(shape) - 1)


def row_of(shape):
    return lax.broadcasted_iota(jnp.int32, shape, len(shape) - 2)


def halves_of(values):
    high = values.astype(jnp.bfloat16).astype(jnp.float32)
    return high, values - high


def thirds_of(values):
    first, rest = halves_of(values)
    second, third = halves_of(rest)
    return first, second, third


def one_of(index, choices, other):
    for at, choice in choices.items():
        other = jnp.where(index == at, choice, other)
    return other


def columns_kernel(
    emb_ref, sketch_ref, points_ref, sketch_t_ref, shift_ref, mean_ref, emb_near, sketch_near, emb_sem, sketch_sem
):
    emb_copy = pltpu.make_async_copy(emb_ref, emb_near, emb_sem)
    sketch_copy = pltpu.make_async_copy(sketch_ref, sketch_near, sketch_sem)
    emb_copy.start()
    sketch_copy.start()
    emb_copy.wait()
    emb = emb_near[...]
    wide = emb.shape[1]
    shift = jnp.sum(emb, axis=1, keepdims=True) * (1.0 / wide)
    shift_ref[...] = jnp.broadcast_to(shift, shift_ref.shape)
    moved = emb - shift
    high, low = halves_of(moved)
    norms = jnp.sum(moved * moved, axis=0, keepdims=True)
    first, second, third = thirds_of(norms)
    at = row_of((16, wide))
    tail = one_of(at, {0: 1.0, 1: 1.0, 2: 1.0, 3: first, 4: second, 5: third}, 0.0)
    points_ref[...] = jnp.concatenate([high, high, low, tail], axis=0).astype(jnp.bfloat16)

    sketch_copy.wait()
    sketch = sketch_near[...]
    mean = jnp.sum(sketch, axis=1, keepdims=True) * (1.0 / wide)
    high, low = halves_of(sketch - mean)
    ones = jnp.where(row_of((8, wide)) == 0, 1.0, 0.0)
    both = jnp.concatenate([high, ones, low, jnp.zeros((LANES - 88, wide), jnp.float32)], axis=0)
    sketch_t_ref[...] = both.T.astype(jnp.bfloat16)
    across = jnp.concatenate(
        [jnp.broadcast_to(mean, (mean.shape[0], LANES)), jnp.zeros((LANES - mean.shape[0], LANES), jnp.float32)], axis=0
    )
    mean_ref[...] = across.T[:8]


def product_kernel(rows_ref, conf_ref, points_ref, sketch_t_ref, shift_ref, mean_ref, out_ref, near_ref, sems):
    row_dev, wide = conf_ref.shape
    copies = []
    for at in range(row_dev // CHUNK):
        part = pl.ds(at * CHUNK, CHUNK)
        copies.append(pltpu.make_async_copy(conf_ref.at[part], near_ref.at[part], sems.at[at]))
        copies[at].start()
    emb = rows_ref[...].reshape(HALF, row_dev)
    moved = emb - shift_ref[:, :1]
    norms = jnp.sum(moved * moved, axis=0, keepdims=True)
    first, second, third = thirds_of(norms)
    high, low = halves_of(-2.0 * moved)
    tail = one_of(row_of((HALF, row_dev)), {0: first, 1: second, 2: third, 3: 1.0, 4: 1.0, 5: 1.0}, 0.0)
    left = jnp.concatenate([high, low, high, tail], axis=0)
    shape = (PACK, LANES)
    lane, row = lane_of(shape), row_of(shape)
    means = jnp.broadcast_to(pltpu.roll(mean_ref[...], HALF, 1)[:1], shape)
    is_mean = (row == ONES + 1 - PACK) & (lane >= HALF)
    for begin in range(0, row_dev, STEP):
        rows = slice(begin, begin + STEP)
        for at in range(begin // CHUNK, (begin + STEP) // CHUNK):
            copies[at].wait()
        near = left[:, rows].T.astype(jnp.bfloat16)[:, :208]
        total = jnp.zeros((STEP, LANES), jnp.float32)
        for start in range(0, wide, 256):
            part = slice(start, start + 256)
            distance = dot(near, points_ref[:, part], ((1,), (0,)))
            weighted = near_ref[rows, part].astype(jnp.float32) * distance
            high = weighted.astype(jnp.bfloat16)
            low = (weighted - high.astype(jnp.float32)).astype(jnp.bfloat16)
            right = sketch_t_ref[part, :]
            total = total + dot(high, right, ((1,), (0,))) + dot(low, right, ((1,), (0,)))
        flat = total.T
        flat = flat[:48] + flat[48:96]
        for tile in range(STEP // LANES):
            top = flat[:PACK, tile * LANES : (tile + 1) * LANES]
            bottom = flat[PACK:, tile * LANES : (tile + 1) * LANES]
            even = jnp.where(lane < HALF, top, pltpu.roll(bottom, HALF, 1))
            odd = jnp.where(lane < HALF, pltpu.roll(top, HALF, 1), bottom)
            at = begin // HALF + 2 * tile
            out_ref[at] = jnp.where(is_mean, means, even)
            out_ref[at + 1] = jnp.where(is_mean, means, odd)


def piece_kernel(got_ref, out_ref):
    total = got_ref[0]
    for block in range(1, got_ref.shape[0]):
        total = total + got_ref[block]
    sums = pltpu.roll(got_ref[:, ONES - PACK, :], HALF, 1)
    means = pltpu.roll(got_ref[:, ONES + 1 - PACK, :], HALF, 1)
    means = means - jnp.sum(means, axis=0, keepdims=True) * (1.0 / means.shape[0])
    fix = dot(means.T, sums, ((1,), (0,)), HIGHEST_PRECISION)
    shape = (PACK, LANES)
    lane, row = lane_of(shape), row_of(shape)
    total = total + jnp.where(lane < HALF, fix[:PACK], pltpu.roll(fix[PACK : 2 * PACK], HALF, 1))
    below = (lane >= HALF) & (row >= ONES - PACK)
    total = jnp.where(below, jnp.where(row == ONES - PACK, 1.0, 0.0), total)
    out_ref[...] = jnp.broadcast_to(total[None], out_ref.shape)


def unpack(pieces_ref):
    lane = lane_of((PACK, LANES))
    tops, bottoms = [], []
    for at in range(0, pieces_ref.shape[0], 2):
        even, odd = pieces_ref[at], pieces_ref[at + 1]
        tops.append(jnp.where(lane < HALF, even, pltpu.roll(odd, HALF, 1)))
        bottoms.append(jnp.where(lane < HALF, pltpu.roll(even, HALF, 1), odd))
    return jnp.concatenate([jnp.concatenate(tops, axis=1), jnp.concatenate(bottoms, axis=1)], axis=0)


def gram_kernel(pieces_ref, out_ref):
    product = unpack(pieces_ref)
    padded = jnp.concatenate([product, jnp.zeros((LANES - 48, product.shape[1]), jnp.float32)], axis=0)
    gram = dot(product, padded, ((1,), (1,)), HIGHEST_PRECISION)
    lane = lane_of((8, LANES))
    packed = jnp.zeros((8, LANES), jnp.float32)
    for group in range(5):
        rows = gram[8 * group : 8 * group + 8]
        lower = jnp.where(lane < 8 * group + 8, rows, 0.0)
        packed = packed + (pltpu.roll(lower, 4 * group * (group + 1), 1) if group else lower)
        packed = packed + pltpu.roll(jnp.where(lane == ONES, rows, 0.0), 120 + group - ONES, 1)
    out_ref[...] = jnp.broadcast_to(packed[None], out_ref.shape)


def spread_lane(rows, at):
    return jnp.broadcast_to(rows[:, at : at + 1], (8, LANES))


def spread_row(rows, at):
    return jnp.broadcast_to(rows[at : at + 1, :], (8, LANES))


def factor_kernel(count, grams_ref, pieces_ref, basis_ref, upper_ref, small_ref):
    packed = grams_ref[0]
    for block in range(1, grams_ref.shape[0]):
        packed = packed + grams_ref[block]
    shape = (8, LANES)
    lane, row = lane_of(shape), row_of(shape)
    lowers, sums = [], []
    for group in range(5):
        back = (LANES - 4 * group * (group + 1)) % LANES
        lower = pltpu.roll(packed, back, 1) if back else packed
        lowers.append(jnp.where(lane < 8 * group + 8, lower, 0.0))
        sums.append(jnp.where(lane == ONES, pltpu.roll(packed, LANES + ONES - 120 - group, 1), 0.0))
    square = jnp.concatenate([a + b for a, b in zip(lowers, sums)] + [jnp.zeros((LANES - 40, LANES), jnp.float32)], axis=0)
    flipped = square.T
    ones_row = jnp.where(lane < ONES, spread_row(flipped[ONES : ONES + 8], 0), jnp.where(lane == INV + ONES, 1.0, 0.0))
    groups, trace = [], jnp.zeros((8, 1), jnp.float32)
    for group in range(5):
        upper = jnp.where((lane >= 8 * group + 8) & (lane < ONES), flipped[8 * group : 8 * group + 8], 0.0)
        full = lowers[group] + upper
        diagonal = lane == 8 * group + row
        trace = trace + jnp.sum(jnp.where(diagonal, full, 0.0), axis=1, keepdims=True)
        full = full + jnp.where(lane == INV + 8 * group + row, 1.0, 0.0)
        groups.append(full - (spread_lane(sums[group], ONES) * (1.0 / count)) * ones_row)

    size = jnp.zeros((8, 1), jnp.float32)
    scaled = []
    for block in range(5):
        base = 8 * block
        columns = {i: [spread_lane(groups[i], base + t) for t in range(8)] for i in range(block, 5)}
        rows = [spread_row(groups[block], t) for t in range(8)]
        entry = {(t, s): spread_row(columns[block][s], t) for t in range(8) for s in range(t, 8)}
        result = jnp.zeros(shape, jnp.float32)
        for t in range(8):
            inverse = 1.0 / entry[t, t]
            for s in range(t + 1, 8):
                factor = entry[t, s] * inverse
                for u in range(s, 8):
                    entry[s, u] = entry[s, u] - factor * entry[t, u]
                rows[s] = rows[s] - factor * rows[t]
            for i in range(block + 1, 5):
                factor = columns[i][t] * inverse
                for s in range(t + 1, 8):
                    columns[i][s] = columns[i][s] - factor * entry[t, s]
                groups[i] = groups[i] - factor * rows[t]
            result = jnp.where(row == t, rows[t] * lax.rsqrt(entry[t, t]), result)
        scaled.append(result)
        kept = (lane >= INV) & (lane < INV + ONES)
        size = size + jnp.sum(jnp.where(kept, result * result, 0.0), axis=1, keepdims=True)
        triangle = jnp.where(lane >= base + row, result, 0.0) * (0.5 / count)
        upper_ref[base : base + 8, :] = triangle[:, :40]
    small_ref[0, 0] = (jnp.sum(trace) * jnp.sum(size) < 2.5 * 40 * 40).astype(jnp.int32)
    solve = jnp.concatenate(scaled, axis=0) * -math.sqrt(count)
    solve = pltpu.roll(solve, LANES - INV, 1)[:, :48]
    basis_ref[...] = dot(solve, unpack(pieces_ref), ((1,), (0,)), HIGHEST_PRECISION)


def call(kernel, outs, flops, *args, **more):
    moved = sum(math.prod(a.shape) * a.dtype.itemsize for a in (*args, *outs))
    return pl.pallas_call(
        kernel,
        out_shape=outs,
        compiler_params=pltpu.CompilerParams(vmem_limit_bytes=VMEM),
        cost_estimate=pl.CostEstimate(flops=flops, bytes_accessed=moved, transcendentals=0),
        **more,
    )(*args)


def array(*shape, dtype=jnp.float32):
    return jax.ShapeDtypeStruct(shape, dtype)


def far(operand):
    return pltpu.with_memory_space_constraint(operand, pltpu.HBM)


def columns_side(embeddings, sketch):
    wide = embeddings.shape[1]
    outs = (
        array(208, wide, dtype=jnp.bfloat16),
        array(wide, LANES, dtype=jnp.bfloat16),
        array(64, LANES),
        array(8, LANES),
    )
    return call(
        columns_kernel,
        outs,
        10_000_000,
        far(embeddings),
        far(sketch),
        in_specs=[pl.BlockSpec(memory_space=pltpu.HBM)] * 2,
        scratch_shapes=[
            pltpu.VMEM(embeddings.shape, jnp.float32),
            pltpu.VMEM(sketch.shape, jnp.float32),
            pltpu.SemaphoreType.DMA,
            pltpu.SemaphoreType.DMA,
        ],
    )


def product_pieces(rows, confidence, sides):
    row_dev, wide = confidence.shape
    outs = (array(row_dev // HALF, PACK, LANES),)
    flops = 2 * row_dev * wide * (256 + 2 * LANES)
    vmem = pl.BlockSpec(memory_space=pltpu.VMEM)
    return call(
        product_kernel,
        outs,
        flops,
        rows,
        far(confidence),
        *sides,
        in_specs=[vmem, pl.BlockSpec(memory_space=pltpu.HBM)] + [vmem] * 4,
        scratch_shapes=[
            pltpu.VMEM(confidence.shape, jnp.bfloat16),
            pltpu.SemaphoreType.DMA((row_dev // CHUNK,)),
        ],
    )[0]


def piece_sum(got):
    return call(piece_kernel, (array(*got.shape),), 1_000_000, got)[0]


def gram_tile(pieces, copies):
    return call(gram_kernel, (array(copies, 8, LANES),), 40_000_000, pieces)[0]


def factored(grams, pieces, count):
    points = pieces.shape[0] * HALF
    outs = (array(40, points), array(40, 40), array(1, 1, dtype=jnp.int32))
    vmem, smem = (pl.BlockSpec(memory_space=space) for space in (pltpu.VMEM, pltpu.SMEM))
    return call(
        functools.partial(factor_kernel, count),
        outs,
        40_000_000,
        grams,
        pieces,
        in_specs=[vmem, vmem],
        out_specs=(vmem, vmem, smem),
    )


def exchange(blocks, axis):
    return lax.all_to_all(blocks, axis, split_axis=0, concat_axis=0, tiled=True)


def target_of(x, y, z_high, z_low, core):
    z = 2 * z_high + z_low
    to_x, to_y = z // 2, 4 * (z % 2) + 2 * core
    to_z = (z + 4 + y - to_y + 8) % 8
    away = (x - to_x + 4) % 4
    half, to_core = away % 2, away // 2
    return (to_x, to_y + half, to_z // 2, to_z % 2, to_core), half, to_z % 2 * 2 + to_core


def flat_index(at, sizes):
    index = 0
    for place, size in zip(at, sizes):
        index = index * size + place
    return index


def local(embeddings, confidence, sketch):
    n_row, n_near = lax.axis_size(ROW), lax.axis_size(NEAR)
    row_dev = confidence.shape[0]
    count = row_dev * n_row

    dims = embeddings.shape[0] // n_near
    sizes = tuple(lax.axis_size(axis) for axis in ROW + COL)
    pairs = []
    for at in itertools.product(*(range(size) for size in sizes)):
        pairs.append((flat_index(at, sizes), flat_index(target_of(*at)[0], sizes)))
    half, part = target_of(*(lax.axis_index(axis) for axis in ROW + COL))[1:]
    mine = lax.dynamic_slice(embeddings, (part * dims, half * row_dev), (dims, row_dev))
    mine = lax.ppermute(mine, ROW + COL, pairs)
    points, sketch_t, shift, mean = columns_side(embeddings, sketch)
    mine, mean = lax.optimization_barrier((mine, mean))
    rows = exchange(jnp.broadcast_to(mine[None], (n_near, dims, row_dev)), NEAR)

    partial_pieces = product_pieces(rows, confidence, (points, sketch_t, shift, mean))
    pieces = exchange(piece_sum(exchange(partial_pieces, COL)), COL)
    grams = exchange(gram_tile(pieces, n_row), ROW)
    basis, upper_tri, small = factored(grams, pieces, count)

    def second_pass(state):
        basis, upper_tri, _ = state
        gram = lax.psum(dot(basis, basis, ((1,), (1,)), HIGHEST_PRECISION), ROW) / count
        factor_low = jnp.linalg.cholesky(gram)
        solved = lax.linalg.triangular_solve(factor_low, basis, left_side=True, lower=True)
        return solved, jnp.dot(factor_low.T, upper_tri, precision=HIGHEST_PRECISION), jnp.int32(1)

    return lax.while_loop(lambda state: state[2] == 0, second_pass, (basis, upper_tri, small[0, 0]))[:2]


def solution(mesh):
    chips = jax.sharding.Mesh(mesh.devices.reshape(4, 8, 4, 2, 2), ROW + COL)
    placed = (P(None, COL), P(ROW, COL), P(None, COL))
    return jax.shard_map(
        local, mesh=chips, in_specs=placed, out_specs=(P(None, ROW), P()), check_vma=False
    )
```

```python
import functools
import itertools
import math

import jax
import jax.numpy as jnp
from jax import lax
from jax.experimental import pallas as pl
from jax.experimental.pallas import tpu as pltpu
from jax.sharding import PartitionSpec as P

HIGHEST_PRECISION = lax.Precision.HIGHEST
ROW, NEAR = ("x", "y"), ("z_low", "core")
COL = ("z_high",) + NEAR
LANES = 128
HALF = 64
PACK = 24
ONES = 40
INV = 48
STEP = 1024
VMEM = 32 * 1024 * 1024


def dot(left, right, contract, precision=None):
    return lax.dot_general(
        left, right, ((contract[0], contract[1]), ((), ())), precision=precision, preferred_element_type=jnp.float32
    )


def lane_of(shape):
    return lax.broadcasted_iota(jnp.int32, shape, len(shape) - 1)


def row_of(shape):
    return lax.broadcasted_iota(jnp.int32, shape, len(shape) - 2)


def halves_of(values):
    high = values.astype(jnp.bfloat16).astype(jnp.float32)
    return high, values - high


def thirds_of(values):
    first, rest = halves_of(values)
    second, third = halves_of(rest)
    return first, second, third


def one_of(index, choices, other):
    for at, choice in choices.items():
        other = jnp.where(index == at, choice, other)
    return other


def columns_kernel(
    emb_ref, sketch_ref, conf_ref, points_ref, sketch_t_ref, shift_ref, mean_ref, conf_near, emb_near, sketch_near, sems
):
    emb_copy = pltpu.make_async_copy(emb_ref, emb_near, sems.at[0])
    sketch_copy = pltpu.make_async_copy(sketch_ref, sketch_near, sems.at[1])
    conf_copy = pltpu.make_async_copy(conf_ref, conf_near, sems.at[2])
    emb_copy.start()
    sketch_copy.start()
    conf_copy.start()
    emb_copy.wait()
    emb = emb_near[...]
    wide = emb.shape[1]
    shift = jnp.sum(emb, axis=1, keepdims=True) * (1.0 / wide)
    shift_ref[...] = jnp.broadcast_to(shift, shift_ref.shape)
    moved = emb - shift
    high, low = halves_of(moved)
    norms = jnp.sum(moved * moved, axis=0, keepdims=True)
    first, second, third = thirds_of(norms)
    at = row_of((16, wide))
    tail = one_of(at, {0: 1.0, 1: 1.0, 2: 1.0, 3: first, 4: second, 5: third}, 0.0)
    points_ref[...] = jnp.concatenate([high, high, low, tail], axis=0).astype(jnp.bfloat16)

    sketch_copy.wait()
    sketch = sketch_near[...]
    mean = jnp.sum(sketch, axis=1, keepdims=True) * (1.0 / wide)
    high, low = halves_of(sketch - mean)
    ones = jnp.where(row_of((8, wide)) == 0, 1.0, 0.0)
    both = jnp.concatenate([high, ones, low, jnp.zeros((LANES - 88, wide), jnp.float32)], axis=0)
    sketch_t_ref[...] = both.T.astype(jnp.bfloat16)
    across = jnp.concatenate(
        [jnp.broadcast_to(mean, (mean.shape[0], LANES)), jnp.zeros((LANES - mean.shape[0], LANES), jnp.float32)], axis=0
    )
    mean_ref[...] = across.T[:8]
    conf_copy.wait()


def product_kernel(rows_ref, conf_ref, points_ref, sketch_t_ref, shift_ref, mean_ref, out_ref):
    row_dev, wide = conf_ref.shape
    emb = rows_ref[...].reshape(HALF, row_dev)
    moved = emb - shift_ref[:, :1]
    norms = jnp.sum(moved * moved, axis=0, keepdims=True)
    first, second, third = thirds_of(norms)
    high, low = halves_of(-2.0 * moved)
    tail = one_of(row_of((HALF, row_dev)), {0: first, 1: second, 2: third, 3: 1.0, 4: 1.0, 5: 1.0}, 0.0)
    left = jnp.concatenate([high, low, high, tail], axis=0)
    shape = (PACK, LANES)
    lane, row = lane_of(shape), row_of(shape)
    means = jnp.broadcast_to(pltpu.roll(mean_ref[...], HALF, 1)[:1], shape)
    is_mean = (row == ONES + 1 - PACK) & (lane >= HALF)
    for begin in range(0, row_dev, STEP):
        rows = slice(begin, begin + STEP)
        near = left[:, rows].T.astype(jnp.bfloat16)[:, :208]
        total = jnp.zeros((STEP, LANES), jnp.float32)
        for start in range(0, wide, 256):
            part = slice(start, start + 256)
            distance = dot(near, points_ref[:, part], ((1,), (0,)))
            weighted = conf_ref[rows, part].astype(jnp.float32) * distance
            high = weighted.astype(jnp.bfloat16)
            low = (weighted - high.astype(jnp.float32)).astype(jnp.bfloat16)
            right = sketch_t_ref[part, :]
            total = total + dot(high, right, ((1,), (0,))) + dot(low, right, ((1,), (0,)))
        flat = total.T
        flat = flat[:48] + flat[48:96]
        for tile in range(STEP // LANES):
            top = flat[:PACK, tile * LANES : (tile + 1) * LANES]
            bottom = flat[PACK:, tile * LANES : (tile + 1) * LANES]
            even = jnp.where(lane < HALF, top, pltpu.roll(bottom, HALF, 1))
            odd = jnp.where(lane < HALF, pltpu.roll(top, HALF, 1), bottom)
            at = begin // HALF + 2 * tile
            out_ref[at] = jnp.where(is_mean, means, even)
            out_ref[at + 1] = jnp.where(is_mean, means, odd)


def piece_kernel(got_ref, out_ref):
    total = got_ref[0]
    for block in range(1, got_ref.shape[0]):
        total = total + got_ref[block]
    sums = pltpu.roll(got_ref[:, ONES - PACK, :], HALF, 1)
    means = pltpu.roll(got_ref[:, ONES + 1 - PACK, :], HALF, 1)
    means = means - jnp.sum(means, axis=0, keepdims=True) * (1.0 / means.shape[0])
    fix = dot(means.T, sums, ((1,), (0,)), HIGHEST_PRECISION)
    shape = (PACK, LANES)
    lane, row = lane_of(shape), row_of(shape)
    total = total + jnp.where(lane < HALF, fix[:PACK], pltpu.roll(fix[PACK : 2 * PACK], HALF, 1))
    below = (lane >= HALF) & (row >= ONES - PACK)
    total = jnp.where(below, jnp.where(row == ONES - PACK, 1.0, 0.0), total)
    out_ref[...] = jnp.broadcast_to(total[None], out_ref.shape)


def unpack(pieces_ref):
    lane = lane_of((PACK, LANES))
    tops, bottoms = [], []
    for at in range(0, pieces_ref.shape[0], 2):
        even, odd = pieces_ref[at], pieces_ref[at + 1]
        tops.append(jnp.where(lane < HALF, even, pltpu.roll(odd, HALF, 1)))
        bottoms.append(jnp.where(lane < HALF, pltpu.roll(even, HALF, 1), odd))
    return jnp.concatenate([jnp.concatenate(tops, axis=1), jnp.concatenate(bottoms, axis=1)], axis=0)


def gram_kernel(pieces_ref, out_ref):
    product = unpack(pieces_ref)
    padded = jnp.concatenate([product, jnp.zeros((LANES - 48, product.shape[1]), jnp.float32)], axis=0)
    gram = dot(product, padded, ((1,), (1,)), HIGHEST_PRECISION)
    lane = lane_of((8, LANES))
    packed = jnp.zeros((8, LANES), jnp.float32)
    for group in range(5):
        rows = gram[8 * group : 8 * group + 8]
        lower = jnp.where(lane < 8 * group + 8, rows, 0.0)
        packed = packed + (pltpu.roll(lower, 4 * group * (group + 1), 1) if group else lower)
        packed = packed + pltpu.roll(jnp.where(lane == ONES, rows, 0.0), 120 + group - ONES, 1)
    out_ref[...] = jnp.broadcast_to(packed[None], out_ref.shape)


def spread_lane(rows, at):
    return jnp.broadcast_to(rows[:, at : at + 1], (8, LANES))


def spread_row(rows, at):
    return jnp.broadcast_to(rows[at : at + 1, :], (8, LANES))


def factor_kernel(count, grams_ref, pieces_ref, basis_ref, upper_ref, small_ref, basis_near, upper_near, sems):
    packed = grams_ref[0]
    for block in range(1, grams_ref.shape[0]):
        packed = packed + grams_ref[block]
    shape = (8, LANES)
    lane, row = lane_of(shape), row_of(shape)
    lowers, sums = [], []
    for group in range(5):
        back = (LANES - 4 * group * (group + 1)) % LANES
        lower = pltpu.roll(packed, back, 1) if back else packed
        lowers.append(jnp.where(lane < 8 * group + 8, lower, 0.0))
        sums.append(jnp.where(lane == ONES, pltpu.roll(packed, LANES + ONES - 120 - group, 1), 0.0))
    square = jnp.concatenate([a + b for a, b in zip(lowers, sums)] + [jnp.zeros((LANES - 40, LANES), jnp.float32)], axis=0)
    flipped = square.T
    ones_row = jnp.where(lane < ONES, spread_row(flipped[ONES : ONES + 8], 0), jnp.where(lane == INV + ONES, 1.0, 0.0))
    groups, trace = [], jnp.zeros((8, 1), jnp.float32)
    for group in range(5):
        upper = jnp.where((lane >= 8 * group + 8) & (lane < ONES), flipped[8 * group : 8 * group + 8], 0.0)
        full = lowers[group] + upper
        diagonal = lane == 8 * group + row
        trace = trace + jnp.sum(jnp.where(diagonal, full, 0.0), axis=1, keepdims=True)
        full = full + jnp.where(lane == INV + 8 * group + row, 1.0, 0.0)
        groups.append(full - (spread_lane(sums[group], ONES) * (1.0 / count)) * ones_row)

    size = jnp.zeros((8, 1), jnp.float32)
    scaled = []
    for block in range(5):
        base = 8 * block
        columns = {i: [spread_lane(groups[i], base + t) for t in range(8)] for i in range(block, 5)}
        rows = [spread_row(groups[block], t) for t in range(8)]
        entry = {(t, s): spread_row(columns[block][s], t) for t in range(8) for s in range(t, 8)}
        result = jnp.zeros(shape, jnp.float32)
        for t in range(8):
            inverse = 1.0 / entry[t, t]
            for s in range(t + 1, 8):
                factor = entry[t, s] * inverse
                for u in range(s, 8):
                    entry[s, u] = entry[s, u] - factor * entry[t, u]
                rows[s] = rows[s] - factor * rows[t]
            for i in range(block + 1, 5):
                factor = columns[i][t] * inverse
                for s in range(t + 1, 8):
                    columns[i][s] = columns[i][s] - factor * entry[t, s]
                groups[i] = groups[i] - factor * rows[t]
            result = jnp.where(row == t, rows[t] * lax.rsqrt(entry[t, t]), result)
        scaled.append(result)
        kept = (lane >= INV) & (lane < INV + ONES)
        size = size + jnp.sum(jnp.where(kept, result * result, 0.0), axis=1, keepdims=True)
        triangle = jnp.where(lane >= base + row, result, 0.0) * (0.5 / count)
        upper_near[base : base + 8, :] = triangle[:, :40]
    upper_copy = pltpu.make_async_copy(upper_near, upper_ref, sems.at[0])
    upper_copy.start()
    solve = jnp.concatenate(scaled, axis=0) * -math.sqrt(count)
    solve = pltpu.roll(solve, LANES - INV, 1)[:, :48]
    basis_near[...] = dot(solve, unpack(pieces_ref), ((1,), (0,)), HIGHEST_PRECISION)
    basis_copy = pltpu.make_async_copy(basis_near, basis_ref, sems.at[1])
    basis_copy.start()
    small_ref[0, 0] = (jnp.sum(trace) * jnp.sum(size) < 2.5 * 40 * 40).astype(jnp.int32)
    upper_copy.wait()
    basis_copy.wait()


def call(kernel, outs, flops, *args, **more):
    moved = sum(math.prod(a.shape) * a.dtype.itemsize for a in (*args, *outs))
    return pl.pallas_call(
        kernel,
        out_shape=outs,
        compiler_params=pltpu.CompilerParams(vmem_limit_bytes=VMEM),
        cost_estimate=pl.CostEstimate(flops=flops, bytes_accessed=moved, transcendentals=0),
        **more,
    )(*args)


def array(*shape, dtype=jnp.float32):
    return jax.ShapeDtypeStruct(shape, dtype)


def far(operand):
    return pltpu.with_memory_space_constraint(operand, pltpu.HBM)


def columns_side(embeddings, sketch, confidence):
    wide = embeddings.shape[1]
    outs = (
        array(208, wide, dtype=jnp.bfloat16),
        array(wide, LANES, dtype=jnp.bfloat16),
        array(64, LANES),
        array(8, LANES),
        pltpu.VMEM(confidence.shape, jnp.bfloat16),
    )
    return call(
        columns_kernel,
        outs,
        10_000_000,
        far(embeddings),
        far(sketch),
        far(confidence),
        in_specs=[pl.BlockSpec(memory_space=pltpu.HBM)] * 3,
        out_specs=(pl.BlockSpec(memory_space=pltpu.VMEM),) * 5,
        scratch_shapes=[
            pltpu.VMEM(embeddings.shape, jnp.float32),
            pltpu.VMEM(sketch.shape, jnp.float32),
            pltpu.SemaphoreType.DMA((3,)),
        ],
    )


def product_pieces(rows, sides):
    points, sketch_t, shift, mean, confidence = sides
    row_dev, wide = confidence.shape
    outs = (array(row_dev // HALF, PACK, LANES),)
    flops = 2 * row_dev * wide * (256 + 2 * LANES)
    confidence = pltpu.with_memory_space_constraint(confidence, pltpu.VMEM)
    return call(product_kernel, outs, flops, rows, confidence, points, sketch_t, shift, mean)[0]


def piece_sum(got):
    return call(piece_kernel, (array(*got.shape),), 1_000_000, got)[0]


def gram_tile(pieces, copies):
    return call(gram_kernel, (array(copies, 8, LANES),), 40_000_000, pieces)[0]


def factored(grams, pieces, count):
    points = pieces.shape[0] * HALF
    outs = (pltpu.HBM((40, points), jnp.float32), pltpu.HBM((40, 40), jnp.float32), array(1, 1, dtype=jnp.int32))
    vmem, smem, hbm = (pl.BlockSpec(memory_space=space) for space in (pltpu.VMEM, pltpu.SMEM, pltpu.HBM))
    return call(
        functools.partial(factor_kernel, count),
        outs,
        40_000_000,
        grams,
        pieces,
        in_specs=[vmem, vmem],
        out_specs=(hbm, hbm, smem),
        scratch_shapes=[
            pltpu.VMEM((40, points), jnp.float32),
            pltpu.VMEM((40, 40), jnp.float32),
            pltpu.SemaphoreType.DMA((2,)),
        ],
    )


def exchange(blocks, axis):
    return lax.all_to_all(blocks, axis, split_axis=0, concat_axis=0, tiled=True)


def target_of(x, y, z_high, z_low, core):
    z = 2 * z_high + z_low
    to_x, to_y = z // 2, 4 * (z % 2) + 2 * core
    to_z = (z + 4 + y - to_y + 8) % 8
    away = (x - to_x + 4) % 4
    half, to_core = away % 2, away // 2
    return (to_x, to_y + half, to_z // 2, to_z % 2, to_core), half, to_z % 2 * 2 + to_core


def flat_index(at, sizes):
    index = 0
    for place, size in zip(at, sizes):
        index = index * size + place
    return index


def local(embeddings, confidence, sketch):
    n_row, n_near = lax.axis_size(ROW), lax.axis_size(NEAR)
    row_dev = confidence.shape[0]
    count = row_dev * n_row

    dims = embeddings.shape[0] // n_near
    sizes = tuple(lax.axis_size(axis) for axis in ROW + COL)
    pairs = []
    for at in itertools.product(*(range(size) for size in sizes)):
        pairs.append((flat_index(at, sizes), flat_index(target_of(*at)[0], sizes)))
    half, part = target_of(*(lax.axis_index(axis) for axis in ROW + COL))[1:]
    mine = lax.dynamic_slice(embeddings, (part * dims, half * row_dev), (dims, row_dev))
    mine = lax.ppermute(mine, ROW + COL, pairs)
    points, sketch_t, shift, mean, near = columns_side(embeddings, sketch, confidence)
    mine, mean = lax.optimization_barrier((mine, mean))
    rows = exchange(jnp.broadcast_to(mine[None], (n_near, dims, row_dev)), NEAR)

    partial_pieces = product_pieces(rows, (points, sketch_t, shift, mean, near))
    pieces = exchange(piece_sum(exchange(partial_pieces, COL)), COL)
    grams = exchange(gram_tile(pieces, n_row), ROW)
    basis, upper_tri, small = factored(grams, pieces, count)

    def second_pass(state):
        basis, upper_tri, _ = state
        gram = lax.psum(dot(basis, basis, ((1,), (1,)), HIGHEST_PRECISION), ROW) / count
        factor_low = jnp.linalg.cholesky(gram)
        solved = lax.linalg.triangular_solve(factor_low, basis, left_side=True, lower=True)
        return solved, jnp.dot(factor_low.T, upper_tri, precision=HIGHEST_PRECISION), jnp.int32(1)

    return lax.while_loop(lambda state: state[2] == 0, second_pass, (basis, upper_tri, small[0, 0]))[:2]


def solution(mesh):
    chips = jax.sharding.Mesh(mesh.devices.reshape(4, 8, 4, 2, 2), ROW + COL)
    placed = (P(None, COL), P(ROW, COL), P(None, COL))
    return jax.shard_map(
        local, mesh=chips, in_specs=placed, out_specs=(P(None, ROW), P()), check_vma=False
    )
```

```python
import functools
import itertools
import math

import jax
import jax.numpy as jnp
from jax import lax
from jax.experimental import pallas as pl
from jax.experimental.pallas import tpu as pltpu
from jax.sharding import PartitionSpec as P

HIGHEST_PRECISION = lax.Precision.HIGHEST
ROW, NEAR = ("x", "y"), ("z_low", "core")
COL = ("z_high",) + NEAR
LANES = 128
HALF = 64
PACK = 24
ONES = 40
INV = 48
STEP = 256
VMEM = 32 * 1024 * 1024


def dot(left, right, contract, precision=None):
    return lax.dot_general(
        left, right, ((contract[0], contract[1]), ((), ())), precision=precision, preferred_element_type=jnp.float32
    )


def lane_of(shape):
    return lax.broadcasted_iota(jnp.int32, shape, len(shape) - 1)


def row_of(shape):
    return lax.broadcasted_iota(jnp.int32, shape, len(shape) - 2)


def halves_of(values):
    high = values.astype(jnp.bfloat16).astype(jnp.float32)
    return high, values - high


def thirds_of(values):
    first, rest = halves_of(values)
    second, third = halves_of(rest)
    return first, second, third


def one_of(index, choices, other):
    for at, choice in choices.items():
        other = jnp.where(index == at, choice, other)
    return other


def columns_kernel(
    emb_ref, sketch_ref, conf_ref, points_ref, sketch_t_ref, shift_ref, mean_ref, conf_near, emb_near, sketch_near, sems
):
    emb_copy = pltpu.make_async_copy(emb_ref, emb_near, sems.at[0])
    sketch_copy = pltpu.make_async_copy(sketch_ref, sketch_near, sems.at[1])
    conf_copy = pltpu.make_async_copy(conf_ref, conf_near, sems.at[2])
    emb_copy.start()
    sketch_copy.start()
    conf_copy.start()
    emb_copy.wait()
    emb = emb_near[...]
    wide = emb.shape[1]
    shift = jnp.sum(emb, axis=1, keepdims=True) * (1.0 / wide)
    shift_ref[...] = jnp.broadcast_to(shift, shift_ref.shape)
    moved = emb - shift
    high, low = halves_of(moved)
    norms = jnp.sum(moved * moved, axis=0, keepdims=True)
    first, second, third = thirds_of(norms)
    at = row_of((16, wide))
    tail = one_of(at, {0: 1.0, 1: 1.0, 2: 1.0, 3: first, 4: second, 5: third}, 0.0)
    points_ref[...] = jnp.concatenate([high, high, low, tail], axis=0).astype(jnp.bfloat16)

    sketch_copy.wait()
    sketch = sketch_near[...]
    mean = jnp.sum(sketch, axis=1, keepdims=True) * (1.0 / wide)
    high, low = halves_of(sketch - mean)
    ones = jnp.where(row_of((8, wide)) == 0, 1.0, 0.0)
    both = jnp.concatenate([high, ones, low, jnp.zeros((LANES - 88, wide), jnp.float32)], axis=0)
    sketch_t_ref[...] = both.T.astype(jnp.bfloat16)
    across = jnp.concatenate(
        [jnp.broadcast_to(mean, (mean.shape[0], LANES)), jnp.zeros((LANES - mean.shape[0], LANES), jnp.float32)], axis=0
    )
    mean_ref[...] = across.T[:8]
    conf_copy.wait()


def product_kernel(rows_ref, conf_ref, points_ref, sketch_t_ref, shift_ref, mean_ref, out_ref):
    row_dev, wide = conf_ref.shape
    emb = rows_ref[...].reshape(HALF, row_dev)
    moved = emb - shift_ref[:, :1]
    norms = jnp.sum(moved * moved, axis=0, keepdims=True)
    first, second, third = thirds_of(norms)
    high, low = halves_of(-2.0 * moved)
    tail = one_of(row_of((HALF, row_dev)), {0: first, 1: second, 2: third, 3: 1.0, 4: 1.0, 5: 1.0}, 0.0)
    left = jnp.concatenate([high, low, high, tail], axis=0)
    shape = (PACK, LANES)
    lane, row = lane_of(shape), row_of(shape)
    means = jnp.broadcast_to(pltpu.roll(mean_ref[...], HALF, 1)[:1], shape)
    is_mean = (row == ONES + 1 - PACK) & (lane >= HALF)
    for begin in range(0, row_dev, STEP):
        rows = slice(begin, begin + STEP)
        near = left[:, rows].T.astype(jnp.bfloat16)[:, :208]
        total = jnp.zeros((STEP, LANES), jnp.float32)
        for start in range(0, wide, 256):
            part = slice(start, start + 256)
            distance = dot(near, points_ref[:, part], ((1,), (0,)))
            weighted = conf_ref[rows, part].astype(jnp.float32) * distance
            high = weighted.astype(jnp.bfloat16)
            low = (weighted - high.astype(jnp.float32)).astype(jnp.bfloat16)
            right = sketch_t_ref[part, :]
            total = total + dot(high, right, ((1,), (0,))) + dot(low, right, ((1,), (0,)))
        flat = total.T
        flat = flat[:48] + flat[48:96]
        for tile in range(STEP // LANES):
            top = flat[:PACK, tile * LANES : (tile + 1) * LANES]
            bottom = flat[PACK:, tile * LANES : (tile + 1) * LANES]
            even = jnp.where(lane < HALF, top, pltpu.roll(bottom, HALF, 1))
            odd = jnp.where(lane < HALF, pltpu.roll(top, HALF, 1), bottom)
            at = begin // HALF + 2 * tile
            out_ref[at] = jnp.where(is_mean, means, even)
            out_ref[at + 1] = jnp.where(is_mean, means, odd)


def piece_kernel(got_ref, out_ref):
    total = got_ref[0]
    for block in range(1, got_ref.shape[0]):
        total = total + got_ref[block]
    sums = pltpu.roll(got_ref[:, ONES - PACK, :], HALF, 1)
    means = pltpu.roll(got_ref[:, ONES + 1 - PACK, :], HALF, 1)
    means = means - jnp.sum(means, axis=0, keepdims=True) * (1.0 / means.shape[0])
    fix = dot(means.T, sums, ((1,), (0,)), HIGHEST_PRECISION)
    shape = (PACK, LANES)
    lane, row = lane_of(shape), row_of(shape)
    total = total + jnp.where(lane < HALF, fix[:PACK], pltpu.roll(fix[PACK : 2 * PACK], HALF, 1))
    below = (lane >= HALF) & (row >= ONES - PACK)
    total = jnp.where(below, jnp.where(row == ONES - PACK, 1.0, 0.0), total)
    out_ref[...] = jnp.broadcast_to(total[None], out_ref.shape)


def unpack(pieces_ref):
    lane = lane_of((PACK, LANES))
    tops, bottoms = [], []
    for at in range(0, pieces_ref.shape[0], 2):
        even, odd = pieces_ref[at], pieces_ref[at + 1]
        tops.append(jnp.where(lane < HALF, even, pltpu.roll(odd, HALF, 1)))
        bottoms.append(jnp.where(lane < HALF, pltpu.roll(even, HALF, 1), odd))
    return jnp.concatenate([jnp.concatenate(tops, axis=1), jnp.concatenate(bottoms, axis=1)], axis=0)


def gram_kernel(pieces_ref, out_ref):
    product = unpack(pieces_ref)
    padded = jnp.concatenate([product, jnp.zeros((LANES - 48, product.shape[1]), jnp.float32)], axis=0)
    gram = dot(product, padded, ((1,), (1,)), HIGHEST_PRECISION)
    lane = lane_of((8, LANES))
    packed = jnp.zeros((8, LANES), jnp.float32)
    for group in range(5):
        rows = gram[8 * group : 8 * group + 8]
        lower = jnp.where(lane < 8 * group + 8, rows, 0.0)
        packed = packed + (pltpu.roll(lower, 4 * group * (group + 1), 1) if group else lower)
        packed = packed + pltpu.roll(jnp.where(lane == ONES, rows, 0.0), 120 + group - ONES, 1)
    out_ref[...] = jnp.broadcast_to(packed[None], out_ref.shape)


def spread_lane(rows, at):
    return jnp.broadcast_to(rows[:, at : at + 1], (8, LANES))


def spread_row(rows, at):
    return jnp.broadcast_to(rows[at : at + 1, :], (8, LANES))


def factor_kernel(count, grams_ref, pieces_ref, basis_ref, upper_ref, small_ref, basis_near, upper_near, sems):
    packed = grams_ref[0]
    for block in range(1, grams_ref.shape[0]):
        packed = packed + grams_ref[block]
    shape = (8, LANES)
    lane, row = lane_of(shape), row_of(shape)
    lowers, sums = [], []
    for group in range(5):
        back = (LANES - 4 * group * (group + 1)) % LANES
        lower = pltpu.roll(packed, back, 1) if back else packed
        lowers.append(jnp.where(lane < 8 * group + 8, lower, 0.0))
        sums.append(jnp.where(lane == ONES, pltpu.roll(packed, LANES + ONES - 120 - group, 1), 0.0))
    square = jnp.concatenate([a + b for a, b in zip(lowers, sums)] + [jnp.zeros((LANES - 40, LANES), jnp.float32)], axis=0)
    flipped = square.T
    ones_row = jnp.where(lane < ONES, spread_row(flipped[ONES : ONES + 8], 0), jnp.where(lane == INV + ONES, 1.0, 0.0))
    groups, trace = [], jnp.zeros((8, 1), jnp.float32)
    for group in range(5):
        upper = jnp.where((lane >= 8 * group + 8) & (lane < ONES), flipped[8 * group : 8 * group + 8], 0.0)
        full = lowers[group] + upper
        diagonal = lane == 8 * group + row
        trace = trace + jnp.sum(jnp.where(diagonal, full, 0.0), axis=1, keepdims=True)
        full = full + jnp.where(lane == INV + 8 * group + row, 1.0, 0.0)
        groups.append(full - (spread_lane(sums[group], ONES) * (1.0 / count)) * ones_row)

    size = jnp.zeros((8, 1), jnp.float32)
    scaled = []
    for block in range(5):
        base = 8 * block
        columns = {i: [spread_lane(groups[i], base + t) for t in range(8)] for i in range(block, 5)}
        rows = [spread_row(groups[block], t) for t in range(8)]
        entry = {(t, s): spread_row(columns[block][s], t) for t in range(8) for s in range(t, 8)}
        result = jnp.zeros(shape, jnp.float32)
        for t in range(8):
            inverse = 1.0 / entry[t, t]
            for s in range(t + 1, 8):
                factor = entry[t, s] * inverse
                for u in range(s, 8):
                    entry[s, u] = entry[s, u] - factor * entry[t, u]
                rows[s] = rows[s] - factor * rows[t]
            for i in range(block + 1, 5):
                factor = columns[i][t] * inverse
                for s in range(t + 1, 8):
                    columns[i][s] = columns[i][s] - factor * entry[t, s]
                groups[i] = groups[i] - factor * rows[t]
            result = jnp.where(row == t, rows[t] * lax.rsqrt(entry[t, t]), result)
        scaled.append(result)
        kept = (lane >= INV) & (lane < INV + ONES)
        size = size + jnp.sum(jnp.where(kept, result * result, 0.0), axis=1, keepdims=True)
        triangle = jnp.where(lane >= base + row, result, 0.0) * (0.5 / count)
        upper_near[base : base + 8, :] = triangle[:, :40]
    upper_copy = pltpu.make_async_copy(upper_near, upper_ref, sems.at[0])
    upper_copy.start()
    solve = jnp.concatenate(scaled, axis=0) * -math.sqrt(count)
    solve = pltpu.roll(solve, LANES - INV, 1)[:, :48]
    product = unpack(pieces_ref)
    basis_copies = []
    for half in range(2):
        part = pl.ds(half * (product.shape[1] // 2), product.shape[1] // 2)
        columns = product[:, half * part.size : (half + 1) * part.size]
        basis_near[:, part] = dot(solve, columns, ((1,), (0,)), HIGHEST_PRECISION)
        basis_copies.append(pltpu.make_async_copy(basis_near.at[:, part], basis_ref.at[:, part], sems.at[1 + half]))
        basis_copies[half].start()
    small_ref[0, 0] = (jnp.sum(trace) * jnp.sum(size) < 2.5 * 40 * 40).astype(jnp.int32)
    upper_copy.wait()
    for copy in basis_copies:
        copy.wait()


def call(kernel, outs, flops, *args, **more):
    moved = sum(math.prod(a.shape) * a.dtype.itemsize for a in (*args, *outs))
    return pl.pallas_call(
        kernel,
        out_shape=outs,
        compiler_params=pltpu.CompilerParams(vmem_limit_bytes=VMEM),
        cost_estimate=pl.CostEstimate(flops=flops, bytes_accessed=moved, transcendentals=0),
        **more,
    )(*args)


def array(*shape, dtype=jnp.float32):
    return jax.ShapeDtypeStruct(shape, dtype)


def far(operand):
    return pltpu.with_memory_space_constraint(operand, pltpu.HBM)


def columns_side(embeddings, sketch, confidence):
    wide = embeddings.shape[1]
    outs = (
        array(208, wide, dtype=jnp.bfloat16),
        array(wide, LANES, dtype=jnp.bfloat16),
        array(64, LANES),
        array(8, LANES),
        pltpu.VMEM(confidence.shape, jnp.bfloat16),
    )
    return call(
        columns_kernel,
        outs,
        10_000_000,
        far(embeddings),
        far(sketch),
        far(confidence),
        in_specs=[pl.BlockSpec(memory_space=pltpu.HBM)] * 3,
        out_specs=(pl.BlockSpec(memory_space=pltpu.VMEM),) * 5,
        scratch_shapes=[
            pltpu.VMEM(embeddings.shape, jnp.float32),
            pltpu.VMEM(sketch.shape, jnp.float32),
            pltpu.SemaphoreType.DMA((3,)),
        ],
    )


def product_pieces(rows, sides):
    points, sketch_t, shift, mean, confidence = sides
    row_dev, wide = confidence.shape
    outs = (array(row_dev // HALF, PACK, LANES),)
    flops = 2 * row_dev * wide * (256 + 2 * LANES)
    confidence = pltpu.with_memory_space_constraint(confidence, pltpu.VMEM)
    return call(product_kernel, outs, flops, rows, confidence, points, sketch_t, shift, mean)[0]


def piece_sum(got):
    return call(piece_kernel, (array(*got.shape),), 1_000_000, got)[0]


def gram_tile(pieces, copies):
    return call(gram_kernel, (array(copies, 8, LANES),), 40_000_000, pieces)[0]


def factored(grams, pieces, count):
    points = pieces.shape[0] * HALF
    outs = (pltpu.HBM((40, points), jnp.float32), pltpu.HBM((40, 40), jnp.float32), array(1, 1, dtype=jnp.int32))
    vmem, smem, hbm = (pl.BlockSpec(memory_space=space) for space in (pltpu.VMEM, pltpu.SMEM, pltpu.HBM))
    return call(
        functools.partial(factor_kernel, count),
        outs,
        40_000_000,
        grams,
        pieces,
        in_specs=[vmem, vmem],
        out_specs=(hbm, hbm, smem),
        scratch_shapes=[
            pltpu.VMEM((40, points), jnp.float32),
            pltpu.VMEM((40, 40), jnp.float32),
            pltpu.SemaphoreType.DMA((3,)),
        ],
    )


def exchange(blocks, axis):
    return lax.all_to_all(blocks, axis, split_axis=0, concat_axis=0, tiled=True)


def target_of(x, y, z_high, z_low, core):
    z = 2 * z_high + z_low
    to_x, to_y = z // 2, 4 * (z % 2) + 2 * core
    to_z = (z + 4 + y - to_y + 8) % 8
    away = (x - to_x + 4) % 4
    half, to_core = away % 2, away // 2
    return (to_x, to_y + half, to_z // 2, to_z % 2, to_core), half, to_z % 2 * 2 + to_core


def flat_index(at, sizes):
    index = 0
    for place, size in zip(at, sizes):
        index = index * size + place
    return index


def local(embeddings, confidence, sketch):
    n_row, n_near = lax.axis_size(ROW), lax.axis_size(NEAR)
    row_dev = confidence.shape[0]
    count = row_dev * n_row

    dims = embeddings.shape[0] // n_near
    sizes = tuple(lax.axis_size(axis) for axis in ROW + COL)
    pairs = []
    for at in itertools.product(*(range(size) for size in sizes)):
        pairs.append((flat_index(at, sizes), flat_index(target_of(*at)[0], sizes)))
    half, part = target_of(*(lax.axis_index(axis) for axis in ROW + COL))[1:]
    mine = lax.dynamic_slice(embeddings, (part * dims, half * row_dev), (dims, row_dev))
    mine = lax.ppermute(mine, ROW + COL, pairs)
    points, sketch_t, shift, mean, near = columns_side(embeddings, sketch, confidence)
    mine, mean = lax.optimization_barrier((mine, mean))
    rows = exchange(jnp.broadcast_to(mine[None], (n_near, dims, row_dev)), NEAR)

    partial_pieces = product_pieces(rows, (points, sketch_t, shift, mean, near))
    pieces = exchange(piece_sum(exchange(partial_pieces, COL)), COL)
    grams = exchange(gram_tile(pieces, n_row), ROW)
    basis, upper_tri, small = factored(grams, pieces, count)

    def second_pass(state):
        basis, upper_tri, _ = state
        gram = lax.psum(dot(basis, basis, ((1,), (1,)), HIGHEST_PRECISION), ROW) / count
        factor_low = jnp.linalg.cholesky(gram)
        solved = lax.linalg.triangular_solve(factor_low, basis, left_side=True, lower=True)
        return solved, jnp.dot(factor_low.T, upper_tri, precision=HIGHEST_PRECISION), jnp.int32(1)

    return lax.while_loop(lambda state: state[2] == 0, second_pass, (basis, upper_tri, small[0, 0]))[:2]


def solution(mesh):
    chips = jax.sharding.Mesh(mesh.devices.reshape(4, 8, 4, 2, 2), ROW + COL)
    placed = (P(None, COL), P(ROW, COL), P(None, COL))
    return jax.shard_map(
        local, mesh=chips, in_specs=placed, out_specs=(P(None, ROW), P()), check_vma=False
    )
```

```python
import functools
import itertools
import math

import jax
import jax.numpy as jnp
from jax import lax
from jax.experimental import pallas as pl
from jax.experimental.pallas import tpu as pltpu
from jax.sharding import PartitionSpec as P

HIGHEST_PRECISION = lax.Precision.HIGHEST
ROW, NEAR = ("x", "y"), ("z_low", "core")
COL = ("z_high",) + NEAR
LANES = 128
HALF = 64
PACK = 24
ONES = 40
INV = 48
STEP = 512
VMEM = 32 * 1024 * 1024


def dot(left, right, contract, precision=None):
    return lax.dot_general(
        left, right, ((contract[0], contract[1]), ((), ())), precision=precision, preferred_element_type=jnp.float32
    )


def lane_of(shape):
    return lax.broadcasted_iota(jnp.int32, shape, len(shape) - 1)


def row_of(shape):
    return lax.broadcasted_iota(jnp.int32, shape, len(shape) - 2)


def halves_of(values):
    high = values.astype(jnp.bfloat16).astype(jnp.float32)
    return high, values - high


def thirds_of(values):
    first, rest = halves_of(values)
    second, third = halves_of(rest)
    return first, second, third


def one_of(index, choices, other):
    for at, choice in choices.items():
        other = jnp.where(index == at, choice, other)
    return other


def columns_kernel(
    emb_ref, sketch_ref, conf_ref, points_ref, sketch_t_ref, shift_ref, mean_ref, conf_near, emb_near, sketch_near, sems
):
    emb_copy = pltpu.make_async_copy(emb_ref, emb_near, sems.at[0])
    sketch_copy = pltpu.make_async_copy(sketch_ref, sketch_near, sems.at[1])
    conf_copy = pltpu.make_async_copy(conf_ref, conf_near, sems.at[2])
    emb_copy.start()
    sketch_copy.start()
    conf_copy.start()
    emb_copy.wait()
    emb = emb_near[...]
    wide = emb.shape[1]
    shift = jnp.sum(emb, axis=1, keepdims=True) * (1.0 / wide)
    shift_ref[...] = jnp.broadcast_to(shift, shift_ref.shape)
    moved = emb - shift
    high, low = halves_of(moved)
    norms = jnp.sum(moved * moved, axis=0, keepdims=True)
    first, second, third = thirds_of(norms)
    at = row_of((16, wide))
    tail = one_of(at, {0: 1.0, 1: 1.0, 2: 1.0, 3: first, 4: second, 5: third}, 0.0)
    points_ref[...] = jnp.concatenate([high, high, low, tail], axis=0).astype(jnp.bfloat16)

    sketch_copy.wait()
    sketch = sketch_near[...]
    mean = jnp.sum(sketch, axis=1, keepdims=True) * (1.0 / wide)
    high, low = halves_of(sketch - mean)
    ones = jnp.where(row_of((8, wide)) == 0, 1.0, 0.0)
    both = jnp.concatenate([high, ones, low, jnp.zeros((LANES - 88, wide), jnp.float32)], axis=0)
    sketch_t_ref[...] = both.T.astype(jnp.bfloat16)
    across = jnp.concatenate(
        [jnp.broadcast_to(mean, (mean.shape[0], LANES)), jnp.zeros((LANES - mean.shape[0], LANES), jnp.float32)], axis=0
    )
    mean_ref[...] = across.T[:8]
    conf_copy.wait()


def product_kernel(rows_ref, conf_ref, points_ref, sketch_t_ref, shift_ref, mean_ref, out_ref):
    row_dev, wide = conf_ref.shape
    emb = rows_ref[...].reshape(HALF, row_dev)
    moved = emb - shift_ref[:, :1]
    norms = jnp.sum(moved * moved, axis=0, keepdims=True)
    first, second, third = thirds_of(norms)
    high, low = halves_of(-2.0 * moved)
    tail = one_of(row_of((HALF, row_dev)), {0: first, 1: second, 2: third, 3: 1.0, 4: 1.0, 5: 1.0}, 0.0)
    left = jnp.concatenate([high, low, high, tail], axis=0)
    shape = (PACK, LANES)
    lane, row = lane_of(shape), row_of(shape)
    means = jnp.broadcast_to(pltpu.roll(mean_ref[...], HALF, 1)[:1], shape)
    is_mean = (row == ONES + 1 - PACK) & (lane >= HALF)
    for begin in range(0, row_dev, STEP):
        rows = slice(begin, begin + STEP)
        near = left[:, rows].T.astype(jnp.bfloat16)[:, :208]
        total = jnp.zeros((STEP, LANES), jnp.float32)
        for start in range(0, wide, 256):
            part = slice(start, start + 256)
            distance = dot(near, points_ref[:, part], ((1,), (0,)))
            weighted = conf_ref[rows, part].astype(jnp.float32) * distance
            high = weighted.astype(jnp.bfloat16)
            low = (weighted - high.astype(jnp.float32)).astype(jnp.bfloat16)
            both = dot(jnp.concatenate([high, low], axis=0), sketch_t_ref[part, :], ((1,), (0,)))
            total = total + both[:STEP] + both[STEP:]
        flat = total.T
        flat = flat[:48] + flat[48:96]
        for tile in range(STEP // LANES):
            top = flat[:PACK, tile * LANES : (tile + 1) * LANES]
            bottom = flat[PACK:, tile * LANES : (tile + 1) * LANES]
            even = jnp.where(lane < HALF, top, pltpu.roll(bottom, HALF, 1))
            odd = jnp.where(lane < HALF, pltpu.roll(top, HALF, 1), bottom)
            at = begin // HALF + 2 * tile
            out_ref[at] = jnp.where(is_mean, means, even)
            out_ref[at + 1] = jnp.where(is_mean, means, odd)


def piece_kernel(got_ref, out_ref):
    total = got_ref[0]
    for block in range(1, got_ref.shape[0]):
        total = total + got_ref[block]
    sums = pltpu.roll(got_ref[:, ONES - PACK, :], HALF, 1)
    means = pltpu.roll(got_ref[:, ONES + 1 - PACK, :], HALF, 1)
    means = means - jnp.sum(means, axis=0, keepdims=True) * (1.0 / means.shape[0])
    fix = dot(means.T, sums, ((1,), (0,)), HIGHEST_PRECISION)
    shape = (PACK, LANES)
    lane, row = lane_of(shape), row_of(shape)
    total = total + jnp.where(lane < HALF, fix[:PACK], pltpu.roll(fix[PACK : 2 * PACK], HALF, 1))
    below = (lane >= HALF) & (row >= ONES - PACK)
    total = jnp.where(below, jnp.where(row == ONES - PACK, 1.0, 0.0), total)
    out_ref[...] = jnp.broadcast_to(total[None], out_ref.shape)


def unpack(pieces_ref):
    lane = lane_of((PACK, LANES))
    tops, bottoms = [], []
    for at in range(0, pieces_ref.shape[0], 2):
        even, odd = pieces_ref[at], pieces_ref[at + 1]
        tops.append(jnp.where(lane < HALF, even, pltpu.roll(odd, HALF, 1)))
        bottoms.append(jnp.where(lane < HALF, pltpu.roll(even, HALF, 1), odd))
    return jnp.concatenate([jnp.concatenate(tops, axis=1), jnp.concatenate(bottoms, axis=1)], axis=0)


def gram_kernel(pieces_ref, out_ref):
    product = unpack(pieces_ref)
    padded = jnp.concatenate([product, jnp.zeros((LANES - 48, product.shape[1]), jnp.float32)], axis=0)
    gram = dot(product, padded, ((1,), (1,)), HIGHEST_PRECISION)
    lane = lane_of((8, LANES))
    packed = jnp.zeros((8, LANES), jnp.float32)
    for group in range(5):
        rows = gram[8 * group : 8 * group + 8]
        lower = jnp.where(lane < 8 * group + 8, rows, 0.0)
        packed = packed + (pltpu.roll(lower, 4 * group * (group + 1), 1) if group else lower)
        packed = packed + pltpu.roll(jnp.where(lane == ONES, rows, 0.0), 120 + group - ONES, 1)
    out_ref[...] = jnp.broadcast_to(packed[None], out_ref.shape)


def spread_lane(rows, at):
    return jnp.broadcast_to(rows[:, at : at + 1], (8, LANES))


def spread_row(rows, at):
    return jnp.broadcast_to(rows[at : at + 1, :], (8, LANES))


def factor_kernel(count, grams_ref, pieces_ref, basis_ref, upper_ref, small_ref, basis_near, upper_near, sems):
    packed = grams_ref[0]
    for block in range(1, grams_ref.shape[0]):
        packed = packed + grams_ref[block]
    shape = (8, LANES)
    lane, row = lane_of(shape), row_of(shape)
    lowers, sums = [], []
    for group in range(5):
        back = (LANES - 4 * group * (group + 1)) % LANES
        lower = pltpu.roll(packed, back, 1) if back else packed
        lowers.append(jnp.where(lane < 8 * group + 8, lower, 0.0))
        sums.append(jnp.where(lane == ONES, pltpu.roll(packed, LANES + ONES - 120 - group, 1), 0.0))
    square = jnp.concatenate([a + b for a, b in zip(lowers, sums)] + [jnp.zeros((LANES - 40, LANES), jnp.float32)], axis=0)
    flipped = square.T
    ones_row = jnp.where(lane < ONES, spread_row(flipped[ONES : ONES + 8], 0), jnp.where(lane == INV + ONES, 1.0, 0.0))
    groups, trace = [], jnp.zeros((8, 1), jnp.float32)
    for group in range(5):
        upper = jnp.where((lane >= 8 * group + 8) & (lane < ONES), flipped[8 * group : 8 * group + 8], 0.0)
        full = lowers[group] + upper
        diagonal = lane == 8 * group + row
        trace = trace + jnp.sum(jnp.where(diagonal, full, 0.0), axis=1, keepdims=True)
        full = full + jnp.where(lane == INV + 8 * group + row, 1.0, 0.0)
        groups.append(full - (spread_lane(sums[group], ONES) * (1.0 / count)) * ones_row)

    size = jnp.zeros((8, 1), jnp.float32)
    scaled = []
    for block in range(5):
        base = 8 * block
        columns = {i: [spread_lane(groups[i], base + t) for t in range(8)] for i in range(block, 5)}
        rows = [spread_row(groups[block], t) for t in range(8)]
        entry = {(t, s): spread_row(columns[block][s], t) for t in range(8) for s in range(t, 8)}
        result = jnp.zeros(shape, jnp.float32)
        for t in range(8):
            inverse = 1.0 / entry[t, t]
            for s in range(t + 1, 8):
                factor = entry[t, s] * inverse
                for u in range(s, 8):
                    entry[s, u] = entry[s, u] - factor * entry[t, u]
                rows[s] = rows[s] - factor * rows[t]
            for i in range(block + 1, 5):
                factor = columns[i][t] * inverse
                for s in range(t + 1, 8):
                    columns[i][s] = columns[i][s] - factor * entry[t, s]
                groups[i] = groups[i] - factor * rows[t]
            result = jnp.where(row == t, rows[t] * lax.rsqrt(entry[t, t]), result)
        scaled.append(result)
        kept = (lane >= INV) & (lane < INV + ONES)
        size = size + jnp.sum(jnp.where(kept, result * result, 0.0), axis=1, keepdims=True)
        triangle = jnp.where(lane >= base + row, result, 0.0) * (0.5 / count)
        upper_near[base : base + 8, :] = triangle[:, :40]
    upper_copy = pltpu.make_async_copy(upper_near, upper_ref, sems.at[0])
    upper_copy.start()
    solve = jnp.concatenate(scaled, axis=0) * -math.sqrt(count)
    solve = pltpu.roll(solve, LANES - INV, 1)[:, :48]
    product = unpack(pieces_ref)
    basis_copies = []
    for half in range(2):
        part = pl.ds(half * (product.shape[1] // 2), product.shape[1] // 2)
        columns = product[:, half * part.size : (half + 1) * part.size]
        basis_near[:, part] = dot(solve, columns, ((1,), (0,)), HIGHEST_PRECISION)
        basis_copies.append(pltpu.make_async_copy(basis_near.at[:, part], basis_ref.at[:, part], sems.at[1 + half]))
        basis_copies[half].start()
    small_ref[0, 0] = (jnp.sum(trace) * jnp.sum(size) < 2.5 * 40 * 40).astype(jnp.int32)
    upper_copy.wait()
    for copy in basis_copies:
        copy.wait()


def call(kernel, outs, flops, *args, **more):
    moved = sum(math.prod(a.shape) * a.dtype.itemsize for a in (*args, *outs))
    return pl.pallas_call(
        kernel,
        out_shape=outs,
        compiler_params=pltpu.CompilerParams(vmem_limit_bytes=VMEM),
        cost_estimate=pl.CostEstimate(flops=flops, bytes_accessed=moved, transcendentals=0),
        **more,
    )(*args)


def array(*shape, dtype=jnp.float32):
    return jax.ShapeDtypeStruct(shape, dtype)


def far(operand):
    return pltpu.with_memory_space_constraint(operand, pltpu.HBM)


def columns_side(embeddings, sketch, confidence):
    wide = embeddings.shape[1]
    outs = (
        array(208, wide, dtype=jnp.bfloat16),
        array(wide, LANES, dtype=jnp.bfloat16),
        array(64, LANES),
        array(8, LANES),
        pltpu.VMEM(confidence.shape, jnp.bfloat16),
    )
    return call(
        columns_kernel,
        outs,
        10_000_000,
        far(embeddings),
        far(sketch),
        far(confidence),
        in_specs=[pl.BlockSpec(memory_space=pltpu.HBM)] * 3,
        out_specs=(pl.BlockSpec(memory_space=pltpu.VMEM),) * 5,
        scratch_shapes=[
            pltpu.VMEM(embeddings.shape, jnp.float32),
            pltpu.VMEM(sketch.shape, jnp.float32),
            pltpu.SemaphoreType.DMA((3,)),
        ],
    )


def product_pieces(rows, sides):
    points, sketch_t, shift, mean, confidence = sides
    row_dev, wide = confidence.shape
    outs = (array(row_dev // HALF, PACK, LANES),)
    flops = 2 * row_dev * wide * (256 + 2 * LANES)
    confidence = pltpu.with_memory_space_constraint(confidence, pltpu.VMEM)
    return call(product_kernel, outs, flops, rows, confidence, points, sketch_t, shift, mean)[0]


def piece_sum(got):
    return call(piece_kernel, (array(*got.shape),), 1_000_000, got)[0]


def gram_tile(pieces, copies):
    return call(gram_kernel, (array(copies, 8, LANES),), 40_000_000, pieces)[0]


def factored(grams, pieces, count):
    points = pieces.shape[0] * HALF
    outs = (pltpu.HBM((40, points), jnp.float32), pltpu.HBM((40, 40), jnp.float32), array(1, 1, dtype=jnp.int32))
    vmem, smem, hbm = (pl.BlockSpec(memory_space=space) for space in (pltpu.VMEM, pltpu.SMEM, pltpu.HBM))
    return call(
        functools.partial(factor_kernel, count),
        outs,
        40_000_000,
        grams,
        pieces,
        in_specs=[vmem, vmem],
        out_specs=(hbm, hbm, smem),
        scratch_shapes=[
            pltpu.VMEM((40, points), jnp.float32),
            pltpu.VMEM((40, 40), jnp.float32),
            pltpu.SemaphoreType.DMA((3,)),
        ],
    )


def exchange(blocks, axis):
    return lax.all_to_all(blocks, axis, split_axis=0, concat_axis=0, tiled=True)


def target_of(x, y, z_high, z_low, core):
    z = 2 * z_high + z_low
    to_x, to_y = z // 2, 4 * (z % 2) + 2 * core
    to_z = (z + 4 + y - to_y + 8) % 8
    away = (x - to_x + 4) % 4
    half, to_core = away % 2, away // 2
    return (to_x, to_y + half, to_z // 2, to_z % 2, to_core), half, to_z % 2 * 2 + to_core


def flat_index(at, sizes):
    index = 0
    for place, size in zip(at, sizes):
        index = index * size + place
    return index


def local(embeddings, confidence, sketch):
    n_row, n_near = lax.axis_size(ROW), lax.axis_size(NEAR)
    row_dev = confidence.shape[0]
    count = row_dev * n_row

    dims = embeddings.shape[0] // n_near
    sizes = tuple(lax.axis_size(axis) for axis in ROW + COL)
    pairs = []
    for at in itertools.product(*(range(size) for size in sizes)):
        pairs.append((flat_index(at, sizes), flat_index(target_of(*at)[0], sizes)))
    half, part = target_of(*(lax.axis_index(axis) for axis in ROW + COL))[1:]
    mine = lax.dynamic_slice(embeddings, (part * dims, half * row_dev), (dims, row_dev))
    mine = lax.ppermute(mine, ROW + COL, pairs)
    points, sketch_t, shift, mean, near = columns_side(embeddings, sketch, confidence)
    mine, mean = lax.optimization_barrier((mine, mean))
    rows = exchange(jnp.broadcast_to(mine[None], (n_near, dims, row_dev)), NEAR)

    partial_pieces = product_pieces(rows, (points, sketch_t, shift, mean, near))
    pieces = exchange(piece_sum(exchange(partial_pieces, COL)), COL)
    grams = exchange(gram_tile(pieces, n_row), ROW)
    basis, upper_tri, small = factored(grams, pieces, count)

    def second_pass(state):
        basis, upper_tri, _ = state
        gram = lax.psum(dot(basis, basis, ((1,), (1,)), HIGHEST_PRECISION), ROW) / count
        factor_low = jnp.linalg.cholesky(gram)
        solved = lax.linalg.triangular_solve(factor_low, basis, left_side=True, lower=True)
        return solved, jnp.dot(factor_low.T, upper_tri, precision=HIGHEST_PRECISION), jnp.int32(1)

    return lax.while_loop(lambda state: state[2] == 0, second_pass, (basis, upper_tri, small[0, 0]))[:2]


def solution(mesh):
    chips = jax.sharding.Mesh(mesh.devices.reshape(4, 8, 4, 2, 2), ROW + COL)
    placed = (P(None, COL), P(ROW, COL), P(None, COL))
    return jax.shard_map(
        local, mesh=chips, in_specs=placed, out_specs=(P(None, ROW), P()), check_vma=False
    )
```

```python
import functools
import itertools
import math

import jax
import jax.numpy as jnp
from jax import lax
from jax.experimental import pallas as pl
from jax.experimental.pallas import tpu as pltpu
from jax.sharding import PartitionSpec as P

HIGHEST_PRECISION = lax.Precision.HIGHEST
ROW, COL = ("x", "y"), ("z", "core")
LANES = 128
HALF = 64
PACK = 24
ONES = 40
INV = 48
STEP = 512
VMEM = 32 * 1024 * 1024


def dot(left, right, contract, precision=None):
    return lax.dot_general(
        left, right, ((contract[0], contract[1]), ((), ())), precision=precision, preferred_element_type=jnp.float32
    )


def lane_of(shape):
    return lax.broadcasted_iota(jnp.int32, shape, len(shape) - 1)


def row_of(shape):
    return lax.broadcasted_iota(jnp.int32, shape, len(shape) - 2)


def halves_of(values):
    high = values.astype(jnp.bfloat16).astype(jnp.float32)
    return high, values - high


def thirds_of(values):
    first, rest = halves_of(values)
    second, third = halves_of(rest)
    return first, second, third


def one_of(index, choices, other):
    for at, choice in choices.items():
        other = jnp.where(index == at, choice, other)
    return other


def columns_kernel(
    emb_ref, sketch_ref, conf_ref, points_ref, sketch_t_ref, shift_ref, mean_ref, conf_near, emb_near, sketch_near, sems
):
    emb_copy = pltpu.make_async_copy(emb_ref, emb_near, sems.at[0])
    sketch_copy = pltpu.make_async_copy(sketch_ref, sketch_near, sems.at[1])
    conf_copy = pltpu.make_async_copy(conf_ref, conf_near, sems.at[2])
    emb_copy.start()
    sketch_copy.start()
    conf_copy.start()
    emb_copy.wait()
    emb = emb_near[...]
    wide = emb.shape[1]
    shift = jnp.sum(emb, axis=1, keepdims=True) * (1.0 / wide)
    shift_ref[...] = jnp.broadcast_to(shift, shift_ref.shape)
    moved = emb - shift
    high, low = halves_of(moved)
    norms = jnp.sum(moved * moved, axis=0, keepdims=True)
    first, second, third = thirds_of(norms)
    at = row_of((16, wide))
    tail = one_of(at, {0: 1.0, 1: 1.0, 2: 1.0, 3: first, 4: second, 5: third}, 0.0)
    points_ref[...] = jnp.concatenate([high, high, low, tail], axis=0).astype(jnp.bfloat16)

    sketch_copy.wait()
    sketch = sketch_near[...]
    mean = jnp.sum(sketch, axis=1, keepdims=True) * (1.0 / wide)
    high, low = halves_of(sketch - mean)
    ones = jnp.where(row_of((8, wide)) == 0, 1.0, 0.0)
    both = jnp.concatenate([high, ones, low, jnp.zeros((LANES - 88, wide), jnp.float32)], axis=0)
    sketch_t_ref[...] = both.T.astype(jnp.bfloat16)
    across = jnp.concatenate(
        [jnp.broadcast_to(mean, (mean.shape[0], LANES)), jnp.zeros((LANES - mean.shape[0], LANES), jnp.float32)], axis=0
    )
    mean_ref[...] = across.T[:8]
    conf_copy.wait()


def product_kernel(rows_ref, conf_ref, points_ref, sketch_t_ref, shift_ref, mean_ref, out_ref):
    row_dev, wide = conf_ref.shape
    emb = rows_ref[...]
    moved = emb - shift_ref[:, :1]
    norms = jnp.sum(moved * moved, axis=0, keepdims=True)
    first, second, third = thirds_of(norms)
    high, low = halves_of(-2.0 * moved)
    tail = one_of(row_of((HALF, row_dev)), {0: first, 1: second, 2: third, 3: 1.0, 4: 1.0, 5: 1.0}, 0.0)
    left = jnp.concatenate([high, low, high, tail], axis=0)
    shape = (PACK, LANES)
    lane, row = lane_of(shape), row_of(shape)
    means = jnp.broadcast_to(pltpu.roll(mean_ref[...], HALF, 1)[:1], shape)
    is_mean = (row == ONES + 1 - PACK) & (lane >= HALF)
    for begin in range(0, row_dev, STEP):
        rows = slice(begin, begin + STEP)
        near = left[:, rows].T.astype(jnp.bfloat16)[:, :208]
        total = jnp.zeros((STEP, LANES), jnp.float32)
        for start in range(0, wide, 256):
            part = slice(start, start + 256)
            distance = dot(near, points_ref[:, part], ((1,), (0,)))
            weighted = conf_ref[rows, part].astype(jnp.float32) * distance
            high = weighted.astype(jnp.bfloat16)
            low = (weighted - high.astype(jnp.float32)).astype(jnp.bfloat16)
            both = dot(jnp.concatenate([high, low], axis=0), sketch_t_ref[part, :], ((1,), (0,)))
            total = total + both[:STEP] + both[STEP:]
        flat = total.T
        flat = flat[:48] + flat[48:96]
        for tile in range(STEP // LANES):
            top = flat[:PACK, tile * LANES : (tile + 1) * LANES]
            bottom = flat[PACK:, tile * LANES : (tile + 1) * LANES]
            even = jnp.where(lane < HALF, top, pltpu.roll(bottom, HALF, 1))
            odd = jnp.where(lane < HALF, pltpu.roll(top, HALF, 1), bottom)
            at = begin // HALF + 2 * tile
            out_ref[at] = jnp.where(is_mean, means, even)
            out_ref[at + 1] = jnp.where(is_mean, means, odd)


def piece_kernel(got_ref, out_ref):
    total = got_ref[0]
    for block in range(1, got_ref.shape[0]):
        total = total + got_ref[block]
    sums = pltpu.roll(got_ref[:, ONES - PACK, :], HALF, 1)
    means = pltpu.roll(got_ref[:, ONES + 1 - PACK, :], HALF, 1)
    means = means - jnp.sum(means, axis=0, keepdims=True) * (1.0 / means.shape[0])
    fix = dot(means.T, sums, ((1,), (0,)), HIGHEST_PRECISION)
    shape = (PACK, LANES)
    lane, row = lane_of(shape), row_of(shape)
    total = total + jnp.where(lane < HALF, fix[:PACK], pltpu.roll(fix[PACK : 2 * PACK], HALF, 1))
    below = (lane >= HALF) & (row >= ONES - PACK)
    total = jnp.where(below, jnp.where(row == ONES - PACK, 1.0, 0.0), total)
    out_ref[...] = jnp.broadcast_to(total[None], out_ref.shape)


def unpack(pieces_ref):
    lane = lane_of((PACK, LANES))
    tops, bottoms = [], []
    for at in range(0, pieces_ref.shape[0], 2):
        even, odd = pieces_ref[at], pieces_ref[at + 1]
        tops.append(jnp.where(lane < HALF, even, pltpu.roll(odd, HALF, 1)))
        bottoms.append(jnp.where(lane < HALF, pltpu.roll(even, HALF, 1), odd))
    return jnp.concatenate([jnp.concatenate(tops, axis=1), jnp.concatenate(bottoms, axis=1)], axis=0)


def gram_kernel(pieces_ref, out_ref):
    product = unpack(pieces_ref)
    padded = jnp.concatenate([product, jnp.zeros((LANES - 48, product.shape[1]), jnp.float32)], axis=0)
    gram = dot(product, padded, ((1,), (1,)), HIGHEST_PRECISION)
    lane = lane_of((8, LANES))
    packed = jnp.zeros((8, LANES), jnp.float32)
    for group in range(5):
        rows = gram[8 * group : 8 * group + 8]
        lower = jnp.where(lane < 8 * group + 8, rows, 0.0)
        packed = packed + (pltpu.roll(lower, 4 * group * (group + 1), 1) if group else lower)
        packed = packed + pltpu.roll(jnp.where(lane == ONES, rows, 0.0), 120 + group - ONES, 1)
    out_ref[...] = jnp.broadcast_to(packed[None], out_ref.shape)


def spread_lane(rows, at):
    return jnp.broadcast_to(rows[:, at : at + 1], (8, LANES))


def spread_row(rows, at):
    return jnp.broadcast_to(rows[at : at + 1, :], (8, LANES))


def factor_kernel(count, grams_ref, pieces_ref, basis_ref, upper_ref, small_ref, basis_near, upper_near, sems):
    packed = grams_ref[0]
    for block in range(1, grams_ref.shape[0]):
        packed = packed + grams_ref[block]
    shape = (8, LANES)
    lane, row = lane_of(shape), row_of(shape)
    lowers, sums = [], []
    for group in range(5):
        back = (LANES - 4 * group * (group + 1)) % LANES
        lower = pltpu.roll(packed, back, 1) if back else packed
        lowers.append(jnp.where(lane < 8 * group + 8, lower, 0.0))
        sums.append(jnp.where(lane == ONES, pltpu.roll(packed, LANES + ONES - 120 - group, 1), 0.0))
    square = jnp.concatenate([a + b for a, b in zip(lowers, sums)] + [jnp.zeros((LANES - 40, LANES), jnp.float32)], axis=0)
    flipped = square.T
    ones_row = jnp.where(lane < ONES, spread_row(flipped[ONES : ONES + 8], 0), jnp.where(lane == INV + ONES, 1.0, 0.0))
    groups, trace = [], jnp.zeros((8, 1), jnp.float32)
    for group in range(5):
        upper = jnp.where((lane >= 8 * group + 8) & (lane < ONES), flipped[8 * group : 8 * group + 8], 0.0)
        full = lowers[group] + upper
        diagonal = lane == 8 * group + row
        trace = trace + jnp.sum(jnp.where(diagonal, full, 0.0), axis=1, keepdims=True)
        full = full + jnp.where(lane == INV + 8 * group + row, 1.0, 0.0)
        groups.append(full - (spread_lane(sums[group], ONES) * (1.0 / count)) * ones_row)

    size = jnp.zeros((8, 1), jnp.float32)
    scaled = []
    for block in range(5):
        base = 8 * block
        columns = {i: [spread_lane(groups[i], base + t) for t in range(8)] for i in range(block, 5)}
        rows = [spread_row(groups[block], t) for t in range(8)]
        entry = {(t, s): spread_row(columns[block][s], t) for t in range(8) for s in range(t, 8)}
        result = jnp.zeros(shape, jnp.float32)
        for t in range(8):
            inverse = 1.0 / entry[t, t]
            for s in range(t + 1, 8):
                factor = entry[t, s] * inverse
                for u in range(s, 8):
                    entry[s, u] = entry[s, u] - factor * entry[t, u]
                rows[s] = rows[s] - factor * rows[t]
            for i in range(block + 1, 5):
                factor = columns[i][t] * inverse
                for s in range(t + 1, 8):
                    columns[i][s] = columns[i][s] - factor * entry[t, s]
                groups[i] = groups[i] - factor * rows[t]
            result = jnp.where(row == t, rows[t] * lax.rsqrt(entry[t, t]), result)
        scaled.append(result)
        kept = (lane >= INV) & (lane < INV + ONES)
        size = size + jnp.sum(jnp.where(kept, result * result, 0.0), axis=1, keepdims=True)
        triangle = jnp.where(lane >= base + row, result, 0.0) * (0.5 / count)
        upper_near[base : base + 8, :] = triangle[:, :40]
    upper_copy = pltpu.make_async_copy(upper_near, upper_ref, sems.at[0])
    upper_copy.start()
    solve = jnp.concatenate(scaled, axis=0) * -math.sqrt(count)
    solve = pltpu.roll(solve, LANES - INV, 1)[:, :48]
    product = unpack(pieces_ref)
    basis_copies = []
    for half in range(2):
        part = pl.ds(half * (product.shape[1] // 2), product.shape[1] // 2)
        columns = product[:, half * part.size : (half + 1) * part.size]
        basis_near[:, part] = dot(solve, columns, ((1,), (0,)), HIGHEST_PRECISION)
        basis_copies.append(pltpu.make_async_copy(basis_near.at[:, part], basis_ref.at[:, part], sems.at[1 + half]))
        basis_copies[half].start()
    small_ref[0, 0] = (jnp.sum(trace) * jnp.sum(size) < 2.5 * 40 * 40).astype(jnp.int32)
    upper_copy.wait()
    for copy in basis_copies:
        copy.wait()


def call(kernel, outs, flops, *args, **more):
    moved = sum(math.prod(a.shape) * a.dtype.itemsize for a in (*args, *outs))
    return pl.pallas_call(
        kernel,
        out_shape=outs,
        compiler_params=pltpu.CompilerParams(vmem_limit_bytes=VMEM),
        cost_estimate=pl.CostEstimate(flops=flops, bytes_accessed=moved, transcendentals=0),
        **more,
    )(*args)


def array(*shape, dtype=jnp.float32):
    return jax.ShapeDtypeStruct(shape, dtype)


def far(operand):
    return pltpu.with_memory_space_constraint(operand, pltpu.HBM)


def columns_side(embeddings, sketch, confidence):
    wide = embeddings.shape[1]
    outs = (
        array(208, wide, dtype=jnp.bfloat16),
        array(wide, LANES, dtype=jnp.bfloat16),
        array(64, LANES),
        array(8, LANES),
        pltpu.VMEM(confidence.shape, jnp.bfloat16),
    )
    return call(
        columns_kernel,
        outs,
        10_000_000,
        far(embeddings),
        far(sketch),
        far(confidence),
        in_specs=[pl.BlockSpec(memory_space=pltpu.HBM)] * 3,
        out_specs=(pl.BlockSpec(memory_space=pltpu.VMEM),) * 5,
        scratch_shapes=[
            pltpu.VMEM(embeddings.shape, jnp.float32),
            pltpu.VMEM(sketch.shape, jnp.float32),
            pltpu.SemaphoreType.DMA((3,)),
        ],
    )


def product_pieces(rows, sides):
    points, sketch_t, shift, mean, confidence = sides
    row_dev, wide = confidence.shape
    outs = (array(row_dev // HALF, PACK, LANES),)
    flops = 2 * row_dev * wide * (256 + 2 * LANES)
    confidence = pltpu.with_memory_space_constraint(confidence, pltpu.VMEM)
    return call(product_kernel, outs, flops, rows, confidence, points, sketch_t, shift, mean)[0]


def piece_sum(got):
    return call(piece_kernel, (array(*got.shape),), 1_000_000, got)[0]


def gram_tile(pieces, copies):
    return call(gram_kernel, (array(copies, 8, LANES),), 40_000_000, pieces)[0]


def factored(grams, pieces, count):
    points = pieces.shape[0] * HALF
    outs = (pltpu.HBM((40, points), jnp.float32), pltpu.HBM((40, 40), jnp.float32), array(1, 1, dtype=jnp.int32))
    vmem, smem, hbm = (pl.BlockSpec(memory_space=space) for space in (pltpu.VMEM, pltpu.SMEM, pltpu.HBM))
    return call(
        functools.partial(factor_kernel, count),
        outs,
        40_000_000,
        grams,
        pieces,
        in_specs=[vmem, vmem],
        out_specs=(hbm, hbm, smem),
        scratch_shapes=[
            pltpu.VMEM((40, points), jnp.float32),
            pltpu.VMEM((40, 40), jnp.float32),
            pltpu.SemaphoreType.DMA((3,)),
        ],
    )


def exchange(blocks, axis):
    return lax.all_to_all(blocks, axis, split_axis=0, concat_axis=0, tiled=True)


def target_of(x, y, z, core):
    to_x, to_y = z // 2, 4 * (z % 2) + 2 * core
    to_z = (z + 4 + y - to_y + 8) % 8
    away = (x - to_x + 4) % 4
    half, to_core = away % 2, away // 2
    return (to_x, to_y + half, to_z, to_core), half


def flat_index(at, sizes):
    index = 0
    for place, size in zip(at, sizes):
        index = index * size + place
    return index


def local(embeddings, confidence, sketch):
    n_row = lax.axis_size(ROW)
    row_dev = confidence.shape[0]
    count = row_dev * n_row

    sizes = tuple(lax.axis_size(axis) for axis in ROW + COL)
    pairs = []
    for at in itertools.product(*(range(size) for size in sizes)):
        pairs.append((flat_index(at, sizes), flat_index(target_of(*at)[0], sizes)))
    half = target_of(*(lax.axis_index(axis) for axis in ROW + COL))[1]
    mine = lax.dynamic_slice_in_dim(embeddings, half * row_dev, row_dev, 1)
    rows = lax.ppermute(mine, ROW + COL, pairs)

    partial_pieces = product_pieces(rows, columns_side(embeddings, sketch, confidence))
    pieces = exchange(piece_sum(exchange(partial_pieces, COL)), COL)
    grams = exchange(gram_tile(pieces, n_row), ROW)
    basis, upper_tri, small = factored(grams, pieces, count)

    def second_pass(state):
        basis, upper_tri, _ = state
        gram = lax.psum(dot(basis, basis, ((1,), (1,)), HIGHEST_PRECISION), ROW) / count
        factor_low = jnp.linalg.cholesky(gram)
        solved = lax.linalg.triangular_solve(factor_low, basis, left_side=True, lower=True)
        return solved, jnp.dot(factor_low.T, upper_tri, precision=HIGHEST_PRECISION), jnp.int32(1)

    return lax.while_loop(lambda state: state[2] == 0, second_pass, (basis, upper_tri, small[0, 0]))[:2]


def solution(mesh):
    chips = jax.sharding.Mesh(mesh.devices.reshape(4, 8, 8, 2), ROW + COL)
    placed = (P(None, COL), P(ROW, COL), P(None, COL))
    return jax.shard_map(
        local, mesh=chips, in_specs=placed, out_specs=(P(None, ROW), P()), check_vma=False
    )
```

```python
import functools
import itertools
import math

import jax
import jax.numpy as jnp
from jax import lax
from jax.experimental import pallas as pl
from jax.experimental.pallas import tpu as pltpu
from jax.sharding import PartitionSpec as P

HIGHEST_PRECISION = lax.Precision.HIGHEST
ROW, NEAR = ("x", "y"), ("z_low", "core")
COL = ("z_high",) + NEAR
LANES = 128
HALF = 64
PACK = 24
ONES = 40
INV = 48
STEP = 512
VMEM = 32 * 1024 * 1024


def dot(left, right, contract, precision=None):
    return lax.dot_general(
        left, right, ((contract[0], contract[1]), ((), ())), precision=precision, preferred_element_type=jnp.float32
    )


def lane_of(shape):
    return lax.broadcasted_iota(jnp.int32, shape, len(shape) - 1)


def row_of(shape):
    return lax.broadcasted_iota(jnp.int32, shape, len(shape) - 2)


def halves_of(values):
    high = values.astype(jnp.bfloat16).astype(jnp.float32)
    return high, values - high


def thirds_of(values):
    first, rest = halves_of(values)
    second, third = halves_of(rest)
    return first, second, third


def one_of(index, choices, other):
    for at, choice in choices.items():
        other = jnp.where(index == at, choice, other)
    return other


def columns_kernel(
    emb_ref, sketch_ref, conf_ref, points_ref, sketch_t_ref, shift_ref, mean_ref, conf_near, emb_near, sketch_near, sems
):
    emb_copy = pltpu.make_async_copy(emb_ref, emb_near, sems.at[0])
    sketch_copy = pltpu.make_async_copy(sketch_ref, sketch_near, sems.at[1])
    conf_copy = pltpu.make_async_copy(conf_ref, conf_near, sems.at[2])
    emb_copy.start()
    sketch_copy.start()
    conf_copy.start()
    emb_copy.wait()
    emb = emb_near[...]
    wide = emb.shape[1]
    shift = jnp.sum(emb, axis=1, keepdims=True) * (1.0 / wide)
    shift_ref[...] = jnp.broadcast_to(shift, shift_ref.shape)
    moved = emb - shift
    high, low = halves_of(moved)
    norms = jnp.sum(moved * moved, axis=0, keepdims=True)
    first, second, third = thirds_of(norms)
    at = row_of((16, wide))
    tail = one_of(at, {0: 1.0, 1: 1.0, 2: 1.0, 3: first, 4: second, 5: third}, 0.0)
    points_ref[...] = jnp.concatenate([high, high, low, tail], axis=0).astype(jnp.bfloat16)

    sketch_copy.wait()
    sketch = sketch_near[...]
    mean = jnp.sum(sketch, axis=1, keepdims=True) * (1.0 / wide)
    high, low = halves_of(sketch - mean)
    ones = jnp.where(row_of((8, wide)) == 0, 1.0, 0.0)
    both = jnp.concatenate([high, ones, low, jnp.zeros((LANES - 88, wide), jnp.float32)], axis=0)
    sketch_t_ref[...] = both.T.astype(jnp.bfloat16)
    across = jnp.concatenate(
        [jnp.broadcast_to(mean, (mean.shape[0], LANES)), jnp.zeros((LANES - mean.shape[0], LANES), jnp.float32)], axis=0
    )
    mean_ref[...] = across.T[:8]
    conf_copy.wait()


def product_kernel(rows_ref, conf_ref, points_ref, sketch_t_ref, shift_ref, mean_ref, out_ref):
    row_dev, wide = conf_ref.shape
    emb = rows_ref[...].reshape(HALF, row_dev)
    moved = emb - shift_ref[:, :1]
    norms = jnp.sum(moved * moved, axis=0, keepdims=True)
    first, second, third = thirds_of(norms)
    high, low = halves_of(-2.0 * moved)
    tail = one_of(row_of((HALF, row_dev)), {0: first, 1: second, 2: third, 3: 1.0, 4: 1.0, 5: 1.0}, 0.0)
    left = jnp.concatenate([high, low, high, tail], axis=0)
    shape = (PACK, LANES)
    lane, row = lane_of(shape), row_of(shape)
    means = jnp.broadcast_to(pltpu.roll(mean_ref[...], HALF, 1)[:1], shape)
    is_mean = (row == ONES + 1 - PACK) & (lane >= HALF)
    nears = [left[:, at : at + STEP].T.astype(jnp.bfloat16)[:, :208] for at in range(0, row_dev, STEP)]
    parts = [slice(start, start + 256) for start in range(0, wide, 256)]
    tiles = [(step, part) for step in range(row_dev // STEP) for part in parts]
    totals = [jnp.zeros((STEP, LANES), jnp.float32) for _ in nears]

    def distances(tile):
        step, part = tile
        return dot(nears[step], points_ref[:, part], ((1,), (0,)))

    ready, split = distances(tiles[0]), None
    for at in range(len(tiles) + 1):
        distance, last = ready, split
        if at + 1 < len(tiles):
            ready = distances(tiles[at + 1])
        if last is not None:
            step, part = tiles[at - 1]
            both = dot(last, sketch_t_ref[part, :], ((1,), (0,)))
            totals[step] = totals[step] + both[:STEP] + both[STEP:]
        if at < len(tiles):
            step, part = tiles[at]
            weighted = conf_ref[step * STEP : (step + 1) * STEP, part].astype(jnp.float32) * distance
            high = weighted.astype(jnp.bfloat16)
            low = (weighted - high.astype(jnp.float32)).astype(jnp.bfloat16)
            split = jnp.concatenate([high, low], axis=0)
    for step, total in enumerate(totals):
        flat = total.T
        flat = flat[:48] + flat[48:96]
        for tile in range(STEP // LANES):
            top = flat[:PACK, tile * LANES : (tile + 1) * LANES]
            bottom = flat[PACK:, tile * LANES : (tile + 1) * LANES]
            even = jnp.where(lane < HALF, top, pltpu.roll(bottom, HALF, 1))
            odd = jnp.where(lane < HALF, pltpu.roll(top, HALF, 1), bottom)
            at = step * (STEP // HALF) + 2 * tile
            out_ref[at] = jnp.where(is_mean, means, even)
            out_ref[at + 1] = jnp.where(is_mean, means, odd)


def piece_kernel(got_ref, out_ref):
    total = got_ref[0]
    for block in range(1, got_ref.shape[0]):
        total = total + got_ref[block]
    sums = pltpu.roll(got_ref[:, ONES - PACK, :], HALF, 1)
    means = pltpu.roll(got_ref[:, ONES + 1 - PACK, :], HALF, 1)
    means = means - jnp.sum(means, axis=0, keepdims=True) * (1.0 / means.shape[0])
    fix = dot(means.T, sums, ((1,), (0,)), HIGHEST_PRECISION)
    shape = (PACK, LANES)
    lane, row = lane_of(shape), row_of(shape)
    total = total + jnp.where(lane < HALF, fix[:PACK], pltpu.roll(fix[PACK : 2 * PACK], HALF, 1))
    below = (lane >= HALF) & (row >= ONES - PACK)
    total = jnp.where(below, jnp.where(row == ONES - PACK, 1.0, 0.0), total)
    out_ref[...] = jnp.broadcast_to(total[None], out_ref.shape)


def unpack(pieces_ref):
    lane = lane_of((PACK, LANES))
    tops, bottoms = [], []
    for at in range(0, pieces_ref.shape[0], 2):
        even, odd = pieces_ref[at], pieces_ref[at + 1]
        tops.append(jnp.where(lane < HALF, even, pltpu.roll(odd, HALF, 1)))
        bottoms.append(jnp.where(lane < HALF, pltpu.roll(even, HALF, 1), odd))
    return jnp.concatenate([jnp.concatenate(tops, axis=1), jnp.concatenate(bottoms, axis=1)], axis=0)


def gram_kernel(pieces_ref, out_ref, product_ref):
    product = unpack(pieces_ref)
    product_ref[...] = product
    padded = jnp.concatenate([product, jnp.zeros((LANES - 48, product.shape[1]), jnp.float32)], axis=0)
    gram = dot(product, padded, ((1,), (1,)), HIGHEST_PRECISION)
    lane = lane_of((8, LANES))
    packed = jnp.zeros((8, LANES), jnp.float32)
    for group in range(5):
        rows = gram[8 * group : 8 * group + 8]
        lower = jnp.where(lane < 8 * group + 8, rows, 0.0)
        packed = packed + (pltpu.roll(lower, 4 * group * (group + 1), 1) if group else lower)
        packed = packed + pltpu.roll(jnp.where(lane == ONES, rows, 0.0), 120 + group - ONES, 1)
    out_ref[...] = jnp.broadcast_to(packed[None], out_ref.shape)


def spread_lane(rows, at):
    return jnp.broadcast_to(rows[:, at : at + 1], (8, LANES))


def spread_row(rows, at):
    return jnp.broadcast_to(rows[at : at + 1, :], (8, LANES))


def factor_kernel(count, grams_ref, product_ref, basis_ref, upper_ref, small_ref, basis_near, upper_near, sems):
    packed = grams_ref[0]
    for block in range(1, grams_ref.shape[0]):
        packed = packed + grams_ref[block]
    shape = (8, LANES)
    lane, row = lane_of(shape), row_of(shape)
    lowers, sums = [], []
    for group in range(5):
        back = (LANES - 4 * group * (group + 1)) % LANES
        lower = pltpu.roll(packed, back, 1) if back else packed
        lowers.append(jnp.where(lane < 8 * group + 8, lower, 0.0))
        sums.append(jnp.where(lane == ONES, pltpu.roll(packed, LANES + ONES - 120 - group, 1), 0.0))
    square = jnp.concatenate([a + b for a, b in zip(lowers, sums)] + [jnp.zeros((LANES - 40, LANES), jnp.float32)], axis=0)
    flipped = square.T
    ones_row = jnp.where(lane < ONES, spread_row(flipped[ONES : ONES + 8], 0), jnp.where(lane == INV + ONES, 1.0, 0.0))
    groups, trace = [], jnp.zeros((8, 1), jnp.float32)
    for group in range(5):
        upper = jnp.where((lane >= 8 * group + 8) & (lane < ONES), flipped[8 * group : 8 * group + 8], 0.0)
        full = lowers[group] + upper
        diagonal = lane == 8 * group + row
        trace = trace + jnp.sum(jnp.where(diagonal, full, 0.0), axis=1, keepdims=True)
        full = full + jnp.where(lane == INV + 8 * group + row, 1.0, 0.0)
        groups.append(full - (spread_lane(sums[group], ONES) * (1.0 / count)) * ones_row)

    size = jnp.zeros((8, 1), jnp.float32)
    scaled = []
    for block in range(5):
        base = 8 * block
        columns = {i: [spread_lane(groups[i], base + t) for t in range(8)] for i in range(block, 5)}
        rows = [spread_row(groups[block], t) for t in range(8)]
        entry = {(t, s): spread_row(columns[block][s], t) for t in range(8) for s in range(t, 8)}
        result = jnp.zeros(shape, jnp.float32)
        for t in range(8):
            inverse = 1.0 / entry[t, t]
            for s in range(t + 1, 8):
                factor = entry[t, s] * inverse
                for u in range(s, 8):
                    entry[s, u] = entry[s, u] - factor * entry[t, u]
                rows[s] = rows[s] - factor * rows[t]
            for i in range(block + 1, 5):
                factor = columns[i][t] * inverse
                for s in range(t + 1, 8):
                    columns[i][s] = columns[i][s] - factor * entry[t, s]
                groups[i] = groups[i] - factor * rows[t]
            result = jnp.where(row == t, rows[t] * lax.rsqrt(entry[t, t]), result)
        scaled.append(result)
        kept = (lane >= INV) & (lane < INV + ONES)
        size = size + jnp.sum(jnp.where(kept, result * result, 0.0), axis=1, keepdims=True)
        triangle = jnp.where(lane >= base + row, result, 0.0) * (0.5 / count)
        upper_near[base : base + 8, :] = triangle[:, :40]
    upper_copy = pltpu.make_async_copy(upper_near, upper_ref, sems.at[0])
    upper_copy.start()
    solve = jnp.concatenate(scaled, axis=0) * -math.sqrt(count)
    solve = pltpu.roll(solve, LANES - INV, 1)[:, :48]
    product = product_ref[...]
    basis_copies = []
    for half in range(2):
        part = pl.ds(half * (product.shape[1] // 2), product.shape[1] // 2)
        columns = product[:, half * part.size : (half + 1) * part.size]
        basis_near[:, part] = dot(solve, columns, ((1,), (0,)), HIGHEST_PRECISION)
        basis_copies.append(pltpu.make_async_copy(basis_near.at[:, part], basis_ref.at[:, part], sems.at[1 + half]))
        basis_copies[half].start()
    small_ref[0, 0] = (jnp.sum(trace) * jnp.sum(size) < 2.5 * 40 * 40).astype(jnp.int32)
    upper_copy.wait()
    for copy in basis_copies:
        copy.wait()


def call(kernel, outs, flops, *args, **more):
    moved = sum(math.prod(a.shape) * a.dtype.itemsize for a in (*args, *outs))
    return pl.pallas_call(
        kernel,
        out_shape=outs,
        compiler_params=pltpu.CompilerParams(vmem_limit_bytes=VMEM),
        cost_estimate=pl.CostEstimate(flops=flops, bytes_accessed=moved, transcendentals=0),
        **more,
    )(*args)


def array(*shape, dtype=jnp.float32):
    return jax.ShapeDtypeStruct(shape, dtype)


def far(operand):
    return pltpu.with_memory_space_constraint(operand, pltpu.HBM)


def columns_side(embeddings, sketch, confidence):
    wide = embeddings.shape[1]
    outs = (
        array(208, wide, dtype=jnp.bfloat16),
        array(wide, LANES, dtype=jnp.bfloat16),
        array(64, LANES),
        array(8, LANES),
        pltpu.VMEM(confidence.shape, jnp.bfloat16),
    )
    return call(
        columns_kernel,
        outs,
        10_000_000,
        far(embeddings),
        far(sketch),
        far(confidence),
        in_specs=[pl.BlockSpec(memory_space=pltpu.HBM)] * 3,
        out_specs=(pl.BlockSpec(memory_space=pltpu.VMEM),) * 5,
        scratch_shapes=[
            pltpu.VMEM(embeddings.shape, jnp.float32),
            pltpu.VMEM(sketch.shape, jnp.float32),
            pltpu.SemaphoreType.DMA((3,)),
        ],
    )


def product_pieces(rows, sides):
    points, sketch_t, shift, mean, confidence = sides
    row_dev, wide = confidence.shape
    outs = (array(row_dev // HALF, PACK, LANES),)
    flops = 2 * row_dev * wide * (256 + 2 * LANES)
    confidence = pltpu.with_memory_space_constraint(confidence, pltpu.VMEM)
    return call(product_kernel, outs, flops, rows, confidence, points, sketch_t, shift, mean)[0]


def piece_sum(got):
    return call(piece_kernel, (array(*got.shape),), 1_000_000, got)[0]


def gram_tile(pieces, copies):
    outs = (array(copies, 8, LANES), array(48, pieces.shape[0] * HALF))
    return call(gram_kernel, outs, 40_000_000, pieces)


def factored(grams, product, count):
    points = product.shape[1]
    outs = (pltpu.HBM((40, points), jnp.float32), pltpu.HBM((40, 40), jnp.float32), array(1, 1, dtype=jnp.int32))
    vmem, smem, hbm = (pl.BlockSpec(memory_space=space) for space in (pltpu.VMEM, pltpu.SMEM, pltpu.HBM))
    return call(
        functools.partial(factor_kernel, count),
        outs,
        40_000_000,
        grams,
        product,
        in_specs=[vmem, vmem],
        out_specs=(hbm, hbm, smem),
        scratch_shapes=[
            pltpu.VMEM((40, points), jnp.float32),
            pltpu.VMEM((40, 40), jnp.float32),
            pltpu.SemaphoreType.DMA((3,)),
        ],
    )


def exchange(blocks, axis):
    return lax.all_to_all(blocks, axis, split_axis=0, concat_axis=0, tiled=True)


def target_of(x, y, z_high, z_low, core):
    z = 2 * z_high + z_low
    to_x, to_y = z // 2, 4 * (z % 2) + 2 * core
    to_z = (z + 4 + y - to_y + 8) % 8
    away = (x - to_x + 4) % 4
    half, to_core = away % 2, away // 2
    return (to_x, to_y + half, to_z // 2, to_z % 2, to_core), half, to_z % 2 * 2 + to_core


def flat_index(at, sizes):
    index = 0
    for place, size in zip(at, sizes):
        index = index * size + place
    return index


def local(embeddings, confidence, sketch):
    n_row, n_near = lax.axis_size(ROW), lax.axis_size(NEAR)
    row_dev = confidence.shape[0]
    count = row_dev * n_row

    dims = embeddings.shape[0] // n_near
    sizes = tuple(lax.axis_size(axis) for axis in ROW + COL)
    pairs = []
    for at in itertools.product(*(range(size) for size in sizes)):
        pairs.append((flat_index(at, sizes), flat_index(target_of(*at)[0], sizes)))
    half, part = target_of(*(lax.axis_index(axis) for axis in ROW + COL))[1:]
    mine = lax.dynamic_slice(embeddings, (part * dims, half * row_dev), (dims, row_dev))
    mine = lax.ppermute(mine, ROW + COL, pairs)
    points, sketch_t, shift, mean, near = columns_side(embeddings, sketch, confidence)
    mine, mean = lax.optimization_barrier((mine, mean))
    rows = exchange(jnp.broadcast_to(mine[None], (n_near, dims, row_dev)), NEAR)

    partial_pieces = product_pieces(rows, (points, sketch_t, shift, mean, near))
    pieces = exchange(piece_sum(exchange(partial_pieces, COL)), COL)
    grams, product = gram_tile(pieces, n_row)
    basis, upper_tri, small = factored(exchange(grams, ROW), product, count)

    def second_pass(state):
        basis, upper_tri, _ = state
        gram = lax.psum(dot(basis, basis, ((1,), (1,)), HIGHEST_PRECISION), ROW) / count
        factor_low = jnp.linalg.cholesky(gram)
        solved = lax.linalg.triangular_solve(factor_low, basis, left_side=True, lower=True)
        return solved, jnp.dot(factor_low.T, upper_tri, precision=HIGHEST_PRECISION), jnp.int32(1)

    return lax.while_loop(lambda state: state[2] == 0, second_pass, (basis, upper_tri, small[0, 0]))[:2]


def solution(mesh):
    chips = jax.sharding.Mesh(mesh.devices.reshape(4, 8, 4, 2, 2), ROW + COL)
    placed = (P(None, COL), P(ROW, COL), P(None, COL))
    return jax.shard_map(
        local, mesh=chips, in_specs=placed, out_specs=(P(None, ROW), P()), check_vma=False
    )
```

```python
import functools
import itertools
import math

import jax
import jax.numpy as jnp
from jax import lax
from jax.experimental import pallas as pl
from jax.experimental.pallas import tpu as pltpu
from jax.sharding import PartitionSpec as P

HIGHEST_PRECISION = lax.Precision.HIGHEST
ROW, NEAR = ("x", "y"), ("z_low", "core")
COL = ("z_high",) + NEAR
LANES = 128
HALF = 64
PACK = 24
ONES = 40
INV = 48
STEP = 512
VMEM = 32 * 1024 * 1024


def dot(left, right, contract, precision=None):
    return lax.dot_general(
        left, right, ((contract[0], contract[1]), ((), ())), precision=precision, preferred_element_type=jnp.float32
    )


def lane_of(shape):
    return lax.broadcasted_iota(jnp.int32, shape, len(shape) - 1)


def row_of(shape):
    return lax.broadcasted_iota(jnp.int32, shape, len(shape) - 2)


def halves_of(values):
    high = values.astype(jnp.bfloat16).astype(jnp.float32)
    return high, values - high


def thirds_of(values):
    first, rest = halves_of(values)
    second, third = halves_of(rest)
    return first, second, third


def one_of(index, choices, other):
    for at, choice in choices.items():
        other = jnp.where(index == at, choice, other)
    return other


def columns_kernel(
    emb_ref, sketch_ref, conf_ref, points_ref, sketch_t_ref, shift_ref, mean_ref, conf_near, emb_near, sketch_near, sems
):
    emb_copy = pltpu.make_async_copy(emb_ref, emb_near, sems.at[0])
    sketch_copy = pltpu.make_async_copy(sketch_ref, sketch_near, sems.at[1])
    conf_copy = pltpu.make_async_copy(conf_ref, conf_near, sems.at[2])
    emb_copy.start()
    sketch_copy.start()
    conf_copy.start()
    emb_copy.wait()
    emb = emb_near[...]
    wide = emb.shape[1]
    shift = jnp.sum(emb, axis=1, keepdims=True) * (1.0 / wide)
    shift_ref[...] = jnp.broadcast_to(shift, shift_ref.shape)
    moved = emb - shift
    high, low = halves_of(moved)
    norms = jnp.sum(moved * moved, axis=0, keepdims=True)
    first, second, third = thirds_of(norms)
    at = row_of((16, wide))
    tail = one_of(at, {0: 1.0, 1: 1.0, 2: 1.0, 3: first, 4: second, 5: third}, 0.0)
    points_ref[...] = jnp.concatenate([high, high, low, tail], axis=0).astype(jnp.bfloat16)

    sketch_copy.wait()
    sketch = sketch_near[...]
    mean = jnp.sum(sketch, axis=1, keepdims=True) * (1.0 / wide)
    high, low = halves_of(sketch - mean)
    ones = jnp.where(row_of((8, wide)) == 0, 1.0, 0.0)
    both = jnp.concatenate([high, ones, low, jnp.zeros((LANES - 88, wide), jnp.float32)], axis=0)
    sketch_t_ref[...] = both.T.astype(jnp.bfloat16)
    across = jnp.concatenate(
        [jnp.broadcast_to(mean, (mean.shape[0], LANES)), jnp.zeros((LANES - mean.shape[0], LANES), jnp.float32)], axis=0
    )
    mean_ref[...] = across.T[:8]
    conf_copy.wait()


def product_kernel(rows_ref, conf_ref, points_ref, sketch_t_ref, shift_ref, mean_ref, out_ref):
    row_dev, wide = conf_ref.shape
    emb = rows_ref[...].reshape(HALF, row_dev)
    moved = emb - shift_ref[:, :1]
    norms = jnp.sum(moved * moved, axis=0, keepdims=True)
    first, second, third = thirds_of(norms)
    high, low = halves_of(-2.0 * moved)
    tail = one_of(row_of((HALF, row_dev)), {0: first, 1: second, 2: third, 3: 1.0, 4: 1.0, 5: 1.0}, 0.0)
    left = jnp.concatenate([high, low, high, tail], axis=0)
    shape = (PACK, LANES)
    lane, row = lane_of(shape), row_of(shape)
    means = jnp.broadcast_to(pltpu.roll(mean_ref[...], HALF, 1)[:1], shape)
    is_mean = (row == ONES + 1 - PACK) & (lane >= HALF)
    nears = [left[:, at : at + STEP].T.astype(jnp.bfloat16)[:, :208] for at in range(0, row_dev, STEP)]
    parts = [slice(start, start + 256) for start in range(0, wide, 256)]
    tiles = [(step, part) for step in range(row_dev // STEP) for part in parts]
    totals = [jnp.zeros((STEP, LANES), jnp.float32) for _ in nears]

    def distances(tile):
        step, part = tile
        return dot(nears[step], points_ref[:, part], ((1,), (0,)))

    ready, split = distances(tiles[0]), None
    for at in range(len(tiles) + 1):
        distance, last = ready, split
        if at + 1 < len(tiles):
            ready = distances(tiles[at + 1])
        if last is not None:
            step, part = tiles[at - 1]
            both = dot(last, sketch_t_ref[part, :], ((1,), (0,)))
            totals[step] = totals[step] + both[:STEP] + both[STEP:]
        if at < len(tiles):
            step, part = tiles[at]
            weighted = conf_ref[step * STEP : (step + 1) * STEP, part].astype(jnp.float32) * distance
            high = weighted.astype(jnp.bfloat16)
            low = (weighted - high.astype(jnp.float32)).astype(jnp.bfloat16)
            split = jnp.concatenate([high, low], axis=0)
    for step, total in enumerate(totals):
        flat = total.T
        flat = flat[:48] + flat[48:96]
        for tile in range(STEP // LANES):
            top = flat[:PACK, tile * LANES : (tile + 1) * LANES]
            bottom = flat[PACK:, tile * LANES : (tile + 1) * LANES]
            even = jnp.where(lane < HALF, top, pltpu.roll(bottom, HALF, 1))
            odd = jnp.where(lane < HALF, pltpu.roll(top, HALF, 1), bottom)
            at = step * (STEP // HALF) + 2 * tile
            out_ref[at] = jnp.where(is_mean, means, even)
            out_ref[at + 1] = jnp.where(is_mean, means, odd)


def piece_kernel(got_ref, out_ref):
    total = got_ref[0]
    for block in range(1, got_ref.shape[0]):
        total = total + got_ref[block]
    sums = pltpu.roll(got_ref[:, ONES - PACK, :], HALF, 1)
    means = pltpu.roll(got_ref[:, ONES + 1 - PACK, :], HALF, 1)
    means = means - jnp.sum(means, axis=0, keepdims=True) * (1.0 / means.shape[0])
    fix = dot(means.T, sums, ((1,), (0,)), HIGHEST_PRECISION)
    shape = (PACK, LANES)
    lane, row = lane_of(shape), row_of(shape)
    total = total + jnp.where(lane < HALF, fix[:PACK], pltpu.roll(fix[PACK : 2 * PACK], HALF, 1))
    below = (lane >= HALF) & (row >= ONES - PACK)
    total = jnp.where(below, jnp.where(row == ONES - PACK, 1.0, 0.0), total)
    out_ref[...] = jnp.broadcast_to(total[None], out_ref.shape)


def unpack(pieces_ref):
    lane = lane_of((PACK, LANES))
    tops, bottoms = [], []
    for at in range(0, pieces_ref.shape[0], 2):
        even, odd = pieces_ref[at], pieces_ref[at + 1]
        tops.append(jnp.where(lane < HALF, even, pltpu.roll(odd, HALF, 1)))
        bottoms.append(jnp.where(lane < HALF, pltpu.roll(even, HALF, 1), odd))
    return jnp.concatenate([jnp.concatenate(tops, axis=1), jnp.concatenate(bottoms, axis=1)], axis=0)


def gram_kernel(pieces_ref, out_ref, product_ref):
    product = unpack(pieces_ref)
    product_ref[...] = product
    padded = jnp.concatenate([product, jnp.zeros((LANES - 48, product.shape[1]), jnp.float32)], axis=0)
    gram = dot(product, padded, ((1,), (1,)), HIGHEST_PRECISION)
    lane = lane_of((8, LANES))
    packed = jnp.zeros((8, LANES), jnp.float32)
    for group in range(5):
        rows = gram[8 * group : 8 * group + 8]
        lower = jnp.where(lane < 8 * group + 8, rows, 0.0)
        packed = packed + (pltpu.roll(lower, 4 * group * (group + 1), 1) if group else lower)
        packed = packed + pltpu.roll(jnp.where(lane == ONES, rows, 0.0), 120 + group - ONES, 1)
    out_ref[...] = jnp.broadcast_to(packed[None], out_ref.shape)


def spread_lane(rows, at):
    return jnp.broadcast_to(rows[:, at : at + 1], (8, LANES))


def spread_row(rows, at):
    return jnp.broadcast_to(rows[at : at + 1, :], (8, LANES))


def factor_kernel(count, grams_ref, product_ref, basis_ref, upper_ref, small_ref, basis_near, upper_near, sems):
    packed = grams_ref[0]
    for block in range(1, grams_ref.shape[0]):
        packed = packed + grams_ref[block]
    shape = (8, LANES)
    lane, row = lane_of(shape), row_of(shape)
    lowers, sums = [], []
    for group in range(5):
        back = (LANES - 4 * group * (group + 1)) % LANES
        lower = pltpu.roll(packed, back, 1) if back else packed
        lowers.append(jnp.where(lane < 8 * group + 8, lower, 0.0))
        sums.append(jnp.where(lane == ONES, pltpu.roll(packed, LANES + ONES - 120 - group, 1), 0.0))
    square = jnp.concatenate([a + b for a, b in zip(lowers, sums)] + [jnp.zeros((LANES - 40, LANES), jnp.float32)], axis=0)
    flipped = square.T
    ones_row = jnp.where(lane < ONES, spread_row(flipped[ONES : ONES + 8], 0), jnp.where(lane == INV + ONES, 1.0, 0.0))
    groups, trace = [], jnp.zeros((8, 1), jnp.float32)
    for group in range(5):
        upper = jnp.where((lane >= 8 * group + 8) & (lane < ONES), flipped[8 * group : 8 * group + 8], 0.0)
        full = lowers[group] + upper
        diagonal = lane == 8 * group + row
        trace = trace + jnp.sum(jnp.where(diagonal, full, 0.0), axis=1, keepdims=True)
        full = full + jnp.where(lane == INV + 8 * group + row, 1.0, 0.0)
        groups.append(full - (spread_lane(sums[group], ONES) * (1.0 / count)) * ones_row)

    size = jnp.zeros((8, 1), jnp.float32)
    scaled = []
    for block in range(5):
        base = 8 * block
        columns = {i: [spread_lane(groups[i], base + t) for t in range(8)] for i in range(block, 5)}
        rows = [spread_row(groups[block], t) for t in range(8)]
        entry = {(t, s): spread_row(columns[block][s], t) for t in range(8) for s in range(t, 8)}
        result = jnp.zeros(shape, jnp.float32)
        for t in range(8):
            inverse = 1.0 / entry[t, t]
            for s in range(t + 1, 8):
                factor = entry[t, s] * inverse
                for u in range(s, 8):
                    entry[s, u] = entry[s, u] - factor * entry[t, u]
                rows[s] = rows[s] - factor * rows[t]
            for i in range(block + 1, 5):
                factor = columns[i][t] * inverse
                for s in range(t + 1, 8):
                    columns[i][s] = columns[i][s] - factor * entry[t, s]
                groups[i] = groups[i] - factor * rows[t]
            result = jnp.where(row == t, rows[t] * lax.rsqrt(entry[t, t]), result)
        scaled.append(result)
        kept = (lane >= INV) & (lane < INV + ONES)
        size = size + jnp.sum(jnp.where(kept, result * result, 0.0), axis=1, keepdims=True)
        triangle = jnp.where(lane >= base + row, result, 0.0) * (0.5 / count)
        upper_near[base : base + 8, :] = triangle[:, :40]
    upper_copy = pltpu.make_async_copy(upper_near, upper_ref, sems.at[0])
    upper_copy.start()
    bound = jnp.sum(trace, axis=0, keepdims=True) * jnp.sum(size, axis=0, keepdims=True)
    small_ref[0, 0] = (bound[0, 0] < 2.5 * 40 * 40).astype(jnp.int32)
    solve = jnp.concatenate(scaled, axis=0) * -math.sqrt(count)
    solve = pltpu.roll(solve, LANES - INV, 1)[:, :48]
    product = product_ref[...]
    basis_copies = []
    for half in range(2):
        part = pl.ds(half * (product.shape[1] // 2), product.shape[1] // 2)
        columns = product[:, half * part.size : (half + 1) * part.size]
        basis_near[:, part] = dot(solve, columns, ((1,), (0,)), HIGHEST_PRECISION)
        basis_copies.append(pltpu.make_async_copy(basis_near.at[:, part], basis_ref.at[:, part], sems.at[1 + half]))
        basis_copies[half].start()
    upper_copy.wait()
    for copy in basis_copies:
        copy.wait()


def call(kernel, outs, flops, *args, **more):
    moved = sum(math.prod(a.shape) * a.dtype.itemsize for a in (*args, *outs))
    return pl.pallas_call(
        kernel,
        out_shape=outs,
        compiler_params=pltpu.CompilerParams(vmem_limit_bytes=VMEM),
        cost_estimate=pl.CostEstimate(flops=flops, bytes_accessed=moved, transcendentals=0),
        **more,
    )(*args)


def array(*shape, dtype=jnp.float32):
    return jax.ShapeDtypeStruct(shape, dtype)


def far(operand):
    return pltpu.with_memory_space_constraint(operand, pltpu.HBM)


def columns_side(embeddings, sketch, confidence):
    wide = embeddings.shape[1]
    outs = (
        array(208, wide, dtype=jnp.bfloat16),
        array(wide, LANES, dtype=jnp.bfloat16),
        array(64, LANES),
        array(8, LANES),
        pltpu.VMEM(confidence.shape, jnp.bfloat16),
    )
    return call(
        columns_kernel,
        outs,
        10_000_000,
        far(embeddings),
        far(sketch),
        far(confidence),
        in_specs=[pl.BlockSpec(memory_space=pltpu.HBM)] * 3,
        out_specs=(pl.BlockSpec(memory_space=pltpu.VMEM),) * 5,
        scratch_shapes=[
            pltpu.VMEM(embeddings.shape, jnp.float32),
            pltpu.VMEM(sketch.shape, jnp.float32),
            pltpu.SemaphoreType.DMA((3,)),
        ],
    )


def product_pieces(rows, sides):
    points, sketch_t, shift, mean, confidence = sides
    row_dev, wide = confidence.shape
    outs = (array(row_dev // HALF, PACK, LANES),)
    flops = 2 * row_dev * wide * (256 + 2 * LANES)
    confidence = pltpu.with_memory_space_constraint(confidence, pltpu.VMEM)
    return call(product_kernel, outs, flops, rows, confidence, points, sketch_t, shift, mean)[0]


def piece_sum(got):
    return call(piece_kernel, (array(*got.shape),), 1_000_000, got)[0]


def gram_tile(pieces, copies):
    outs = (array(copies, 8, LANES), array(48, pieces.shape[0] * HALF))
    return call(gram_kernel, outs, 40_000_000, pieces)


def factored(grams, product, count):
    points = product.shape[1]
    outs = (pltpu.HBM((40, points), jnp.float32), pltpu.HBM((40, 40), jnp.float32), array(1, 1, dtype=jnp.int32))
    vmem, smem, hbm = (pl.BlockSpec(memory_space=space) for space in (pltpu.VMEM, pltpu.SMEM, pltpu.HBM))
    return call(
        functools.partial(factor_kernel, count),
        outs,
        40_000_000,
        grams,
        product,
        in_specs=[vmem, vmem],
        out_specs=(hbm, hbm, smem),
        scratch_shapes=[
            pltpu.VMEM((40, points), jnp.float32),
            pltpu.VMEM((40, 40), jnp.float32),
            pltpu.SemaphoreType.DMA((3,)),
        ],
    )


def exchange(blocks, axis):
    return lax.all_to_all(blocks, axis, split_axis=0, concat_axis=0, tiled=True)


def target_of(x, y, z_high, z_low, core):
    z = 2 * z_high + z_low
    to_x, to_y = z // 2, 4 * (z % 2) + 2 * core
    to_z = (z + 4 + y - to_y + 8) % 8
    away = (x - to_x + 4) % 4
    half, to_core = away % 2, away // 2
    return (to_x, to_y + half, to_z // 2, to_z % 2, to_core), half, to_z % 2 * 2 + to_core


def flat_index(at, sizes):
    index = 0
    for place, size in zip(at, sizes):
        index = index * size + place
    return index


def local(embeddings, confidence, sketch):
    n_row, n_near = lax.axis_size(ROW), lax.axis_size(NEAR)
    row_dev = confidence.shape[0]
    count = row_dev * n_row

    dims = embeddings.shape[0] // n_near
    sizes = tuple(lax.axis_size(axis) for axis in ROW + COL)
    pairs = []
    for at in itertools.product(*(range(size) for size in sizes)):
        pairs.append((flat_index(at, sizes), flat_index(target_of(*at)[0], sizes)))
    half, part = target_of(*(lax.axis_index(axis) for axis in ROW + COL))[1:]
    mine = lax.dynamic_slice(embeddings, (part * dims, half * row_dev), (dims, row_dev))
    mine = lax.ppermute(mine, ROW + COL, pairs)
    points, sketch_t, shift, mean, near = columns_side(embeddings, sketch, confidence)
    mine, mean = lax.optimization_barrier((mine, mean))
    rows = exchange(jnp.broadcast_to(mine[None], (n_near, dims, row_dev)), NEAR)

    partial_pieces = product_pieces(rows, (points, sketch_t, shift, mean, near))
    pieces = exchange(piece_sum(exchange(partial_pieces, COL)), COL)
    grams, product = gram_tile(pieces, n_row)
    basis, upper_tri, small = factored(exchange(grams, ROW), product, count)

    def second_pass(state):
        basis, upper_tri, _ = state
        gram = lax.psum(dot(basis, basis, ((1,), (1,)), HIGHEST_PRECISION), ROW) / count
        factor_low = jnp.linalg.cholesky(gram)
        solved = lax.linalg.triangular_solve(factor_low, basis, left_side=True, lower=True)
        return solved, jnp.dot(factor_low.T, upper_tri, precision=HIGHEST_PRECISION), jnp.int32(1)

    return lax.while_loop(lambda state: state[2] == 0, second_pass, (basis, upper_tri, small[0, 0]))[:2]


def solution(mesh):
    chips = jax.sharding.Mesh(mesh.devices.reshape(4, 8, 4, 2, 2), ROW + COL)
    placed = (P(None, COL), P(ROW, COL), P(None, COL))
    return jax.shard_map(
        local, mesh=chips, in_specs=placed, out_specs=(P(None, ROW), P()), check_vma=False
    )
```
